32 devices in a mesh: row: 8 (over y, x, core), col: 4 (over z).
Axes of the slice: x: 2, y: 2, z: 4, core: 2. Of those that a mesh axis runs over, the one named last changes fastest.
Arguments:
- p_blocks: bfloat16 [1536, 128, 128], P(('row', 'col')), may hold values from -6 to 6
- p_positions: int32 [1536], P(('row', 'col')), may hold values from 0 to 127, as said below
- h_blocks: bfloat16 [32, 128, 128], P('col'), may hold values from -0.1875 to 0.1875
- h_rows: int32 [32], replicated, may hold values from 0 to 63, as said below
- keep_mask: int32 [64, 4], P(('row', 'col')), may hold values 0 or 1
- owner_ids: int32 [64, 4, 1], P(('row', 'col')), may hold values from 0 to 7; in each aligned block of 8 rows (0 to 7, 8 to 15, ..., all dimensions but the last counted through in order) at most 2 rows name the same one
Outputs:
- owned: bfloat16 [256, 2, 128, 128], P(('row', 'col'))
The draws below stay inside these ranges and needn't reach their ends.
Inputs may be any that keep to these rules, and one draw needn't show every extreme that they name: `p_positions`: within each group of 48 entries no value repeats. `h_rows`: within each group of 8 entries no value repeats. `owner_ids`: among the 8 blocks of one group of 2 block rows no owner appears more than 2 times.
All inputs are finite; a program needn't handle non-finite values. No bound on the sum of `keep_mask` on one device may be relied on, other than what follows from the above.
Results may differ from the reference program's by a relative error of at most 0.012.
Values may be sent and summed in bfloat16 or wider, within the bound.
A program may use at most 64 MiB of HBM per device.

```python
import math
import jax
import jax.numpy as jnp
import numpy as np
from jax import lax

BLOCK = 128
RB = 2
KB = 64
NH = 8
NP = 48
SEND_CAP = 2
NRG = 8
NCB = 4
NBR = 64


def draw_p_positions(key, part):
    key = jax.random.fold_in(key, 11)
    keys = jax.random.split(key, NRG * NCB)
    orders = jax.vmap(lambda single: jax.random.permutation(single, RB * KB))(keys)
    return orders[:, :NP].reshape(-1).astype(jnp.int32)


def draw_h_rows(key, part):
    key = jax.random.fold_in(key, 23)
    keys = jax.random.split(key, NCB)
    orders = jax.vmap(lambda single: jax.random.permutation(single, KB))(keys)
    return orders[:, :NH].reshape(-1).astype(jnp.int32)


def with_ends(values, stream_key, smallest, high):
    extent = values.shape
    place = [jax.random.randint(jax.random.fold_in(stream_key, axis), (), 0, extent[axis]) for axis in range(len(extent))]
    values = values.at[tuple(place)].set(smallest)
    longest = extent.index(max(extent))
    place[longest] = (place[longest] + 1) % extent[longest]
    return values.at[tuple(place)].set(high)


def block_scale(rng, extent, pieces, least, largest):
    factor_of, own = 1.0, jax.random.fold_in(rng, 6)
    for axis_at, shards_of in pieces:
        draws = jnp.exp(jax.random.uniform(jax.random.fold_in(own, axis_at), (shards_of,), jnp.float32, least / len(pieces), largest / len(pieces)))
        factor_of = factor_of * jnp.repeat(draws, extent[axis_at] // shards_of).reshape([-1 if axis == axis_at else 1 for axis in range(len(extent))])
    return factor_of


def deal_out(own_key, own, number, rows, amount, top, limit, skew):
    order = jax.random.permutation(own_key, amount)
    crowded, usual = shares(amount, rows * top, limit, skew, True), shares(amount, rows * top, limit, skew, False)
    places = jnp.arange(amount)

    def named(tallies, turn):
        used = int((tallies > 0).sum())
        fixed = max(1, used // 4)
        shifted = fixed + (places - fixed + turn * (used - fixed)) % max(1, amount - fixed)
        return jnp.zeros((amount,), jnp.int32).at[order[jnp.where(places < fixed, places, shifted)]].set(jnp.asarray(tallies, jnp.int32))

    tallies = jnp.where(number % 4 == 0, named(crowded, number // 4), named(usual, number - number // 4 - 1))
    mixed = jax.random.permutation(jax.random.fold_in(own, 3), amount)
    source_of, sink = mixed[0:amount // 2 * 2:2], mixed[1:amount // 2 * 2:2]
    slack = jnp.minimum(tallies[source_of] - 1, limit - tallies[sink]) // 2
    slack = jnp.where((source_of == order[0]) | (sink == order[0]) | (tallies[sink] == 0), 0, jnp.maximum(slack, 0))
    shifted = jax.random.randint(jax.random.fold_in(own, 4), (amount // 2,), 0, 1 << 20) % (slack + 1)
    tallies = tallies.at[source_of].add(-shifted).at[sink].add(shifted)
    members = jnp.searchsorted(jnp.cumsum(tallies), jnp.arange(rows * top), side="right").astype(jnp.int32)
    grid = members.reshape(top, rows).T
    grid = grid[jax.random.permutation(jax.random.fold_in(own, 1), rows)]
    turn = jax.random.randint(jax.random.fold_in(own, 2), (rows, 1), 0, top)
    return jnp.take_along_axis(grid, (jnp.arange(top)[None, :] + turn) % top, axis=1)


def shares(number_of, total, reach, skew, full):
    loads = [(1 << 20) // math.isqrt(rank ** skew) + 1 for rank in range(1, number_of + 1)]
    largest = reach if full else min(reach, max(-(-total // number_of), total * loads[0] // sum(loads)))
    least = 1 if total - largest >= number_of - 1 else 0
    holding, surplus = [largest] + [least] * (number_of - 1), total - largest - least * (number_of - 1)
    while surplus > 0:
        movable = [i for i in range(1, number_of) if holding[i] < largest] or [i for i in range(1, number_of) if holding[i] < reach]
        whole, budget = sum([loads[i] for i in movable]), surplus
        for i in movable:
            extra = min(reach - holding[i], max(1, budget * loads[i] // whole), surplus)
            holding[i] = holding[i] + extra
            surplus = surplus - extra
    return np.array(holding)


def scatter_about(key, extent, scale, bound, shards=(), kind=jnp.bfloat16):
    entries = jax.random.normal(key, extent, jnp.float32) * scale
    if len(shards) > 0:
        entries = block_scale(key, extent, shards, -0.22, 0.18) * entries
    return jnp.clip(entries, min=-bound, max=bound).astype(kind)


def setup_inputs(seed: int = 0) -> dict:
    splits = jax.random.split(jax.random.key(seed), 7)
    p_blocks = scatter_about(splits[0], (NP * NRG * NCB, BLOCK, BLOCK), 1.0, 6.0, ((0, 32),))
    p_positions = draw_p_positions(jax.random.fold_in(splits[6], 71), 0)
    h_blocks = scatter_about(splits[2], (NH * NCB, BLOCK, BLOCK), (NH * BLOCK) ** -0.5, 0.1875, ((0, 4),))
    h_rows = draw_h_rows(jax.random.fold_in(splits[6], 71), 0)
    keep_mask = with_ends((jax.random.randint(splits[4], (NBR, NCB), 0, 3) < 2).astype(jnp.int32), jax.random.fold_in(splits[4], 1), 0, 1)
    owner_ids_keys = jax.random.split(jax.random.fold_in(splits[5], 1), NBR * NCB // (RB * NCB))
    owner_ids_turns = jax.random.permutation(jax.random.fold_in(splits[5], 3), NBR * NCB // (RB * NCB))
    owner_ids = jax.vmap(lambda own, number: deal_out(jax.random.fold_in(splits[5], 2), own, number, RB * NCB, NRG, 1, SEND_CAP, 2))(owner_ids_keys, owner_ids_turns).reshape((NBR, NCB, 1))
    return {"p_blocks": p_blocks, "p_positions": p_positions, "h_blocks": h_blocks, "h_rows": h_rows, "keep_mask": keep_mask, "owner_ids": owner_ids}


def reference(p_blocks, p_positions, h_blocks, h_rows, keep_mask, owner_ids):
    groups = NRG * NCB
    block_size = BLOCK
    p_values = p_blocks.reshape(groups, NP, block_size, block_size)
    p_where = p_positions.reshape(groups, NP)
    h_values = h_blocks.astype(jnp.float32).reshape(NCB, NH, block_size, block_size)

    def device_product(inputs):
        values_in, index_in = inputs
        slot_ids = (index_in % KB) * RB + index_in // KB
        dense_panel = jnp.zeros((KB * RB, block_size, block_size), jnp.float32)
        dense_panel = dense_panel.at[slot_ids].set(values_in.astype(jnp.float32))
        dense_panel = dense_panel.reshape(KB, RB, block_size, block_size)
        columns = dense_panel[h_rows].reshape(NCB, NH, RB, block_size, block_size)
        product = jnp.einsum('jnrab,jnbc->rjac', columns, h_values)
        return product.astype(jnp.bfloat16)

    blocks = lax.map(device_product, (p_values, p_where))
    keep_flags = keep_mask.reshape(groups, RB, NCB) == 1
    blocks = jnp.where(keep_flags[:, :, :, None, None], blocks, jnp.zeros_like(blocks))
    blocks = blocks.reshape(groups * RB * NCB, block_size, block_size)
    target_owner = owner_ids.reshape(groups, RB * NCB).astype(jnp.int32)
    onehot = (target_owner[:, :, None] == jnp.arange(NRG, dtype=jnp.int32)[None, None, :]).astype(jnp.int32)
    rank_of = jnp.sum((jnp.cumsum(onehot, axis=1) - onehot) * onehot, axis=2).astype(jnp.int32)
    group_ids = jnp.arange(groups, dtype=jnp.int32)[:, None]
    target = (target_owner * NCB + group_ids % NCB) * NRG + group_ids // NCB
    owned = jnp.zeros((NRG * NRG * NCB, SEND_CAP, block_size, block_size), jnp.bfloat16)
    owned = owned.at[target.reshape(-1), rank_of.reshape(-1)].set(blocks)
    return owned
```

```python
import functools

import jax
import jax.numpy as jnp
from jax import lax
from jax.experimental import pallas as pl
from jax.experimental.pallas import tpu as pltpu
from jax.sharding import PartitionSpec as P

KB = 64
SEND_CAP = 2
LANES = 128
UNROLL = 64
MESH = pl.DeviceIdType.MESH


def repeat(count, body, init=None):
    if count <= UNROLL:
        for i in range(count):
            init = body(i, init)
        return init
    return lax.fori_loop(0, count, body, init)


def flip(value, stride):
    bit = lax.rem(lax.div(value, stride), 2)
    return value + stride * (1 - 2 * bit)


def xor(value, mask):
    bit = 1
    while bit <= mask:
        if mask & bit:
            value = flip(value, jnp.int32(bit))
        bit *= 2
    return value


def kernel(
    rows, cols, pos_ref, hrow_ref, keep_ref, owner_ref, p_ref, h_ref, out_ref,
    pv, hall, kept, outgoing, table, stable,
    local_sem, move_send, move_recv, core_send, core_recv, deal_send, deal_recv,
):
    me_r, me_c = lax.axis_index("row"), lax.axis_index("col")
    core = lax.rem(me_r, 2)
    listed_p = p_ref.shape[0]
    block = p_ref.shape[-1]
    rb, ncb = keep_ref.shape
    blocks = rb * ncb
    listed_h = hrow_ref.shape[0] // cols
    dims = rows.bit_length() - 2
    places = 2**dims
    power = cols & (cols - 1) == 0

    def target(step):
        return xor(me_c, step) if power else lax.rem(me_c + step, cols)

    def origin(step):
        return xor(me_c, step) if power else lax.rem(me_c + cols - step, cols)

    strides = []
    for i in range(dims):
        first, second = 2 ** (dims - i), 2 ** (i + 1)
        strides.append(first + core * (second - first))
    pieces = [me_r]
    for stride in strides:
        pieces = pieces + [flip(piece, stride) for piece in pieces]
    partner = flip(me_r, jnp.int32(1))

    p_copy = pltpu.make_async_copy(p_ref, pv.at[pl.ds(0, listed_p)], local_sem.at[0])
    h_copy = pltpu.make_async_copy(h_ref, hall.at[me_c], local_sem.at[1])
    p_copy.start()
    h_copy.start()

    barrier = pltpu.get_barrier_semaphore()
    for step in range(1, cols):
        pl.semaphore_signal(barrier, inc=1, device_id=(me_r, target(step)), device_id_type=MESH)
    for step in range(1, rows):
        pl.semaphore_signal(barrier, inc=1, device_id=(xor(me_r, step), me_c), device_id_type=MESH)
    pl.semaphore_wait(barrier, cols + rows - 2)

    def first_copy(step):
        return pltpu.make_async_remote_copy(
            src_ref=h_ref.at[me_r], dst_ref=hall.at[me_c, me_r],
            send_sem=move_send.at[step, 0], recv_sem=move_recv.at[step, 0],
            device_id=(me_r, target(step)), device_id_type=MESH,
        )

    def plane_copy(step, place, onto, to_row, sends, recvs):
        piece = hall.at[origin(step), pieces[place]]
        return pltpu.make_async_remote_copy(
            src_ref=piece, dst_ref=piece,
            send_sem=sends.at[step, onto], recv_sem=recvs.at[step, onto],
            device_id=(to_row, me_c), device_id_type=MESH,
        )

    def core_copy(step, place):
        return plane_copy(step, place, place, partner, core_send, core_recv)

    for step in range(1, cols):
        first_copy(step).start()

    width = table.shape[-1]
    lane = lax.broadcasted_iota(jnp.int32, (8, width), 1)
    line = lax.broadcasted_iota(jnp.int32, (8, width), 0)
    wanted = repeat(
        hrow_ref.shape[0], lambda m, held: jnp.where(lane == m, hrow_ref[m], held),
        jnp.full((8, width), -1, jnp.int32),
    )
    wanted = jnp.where(wanted < 0, -1, wanted + line * KB)
    table[0] = repeat(
        listed_p, lambda q, held: jnp.where(wanted == pos_ref[q], q, held),
        jnp.full((8, width), listed_p, jnp.int32),
    )
    filled = jnp.full((8, width), blocks, jnp.int32)
    count = jnp.zeros((8, width), jnp.int32)
    for b in range(blocks):
        r, j = b // ncb, b % ncb
        hit = lane == owner_ref[r, j, 0]
        taken = jnp.where(keep_ref[r, j] == 1, b, blocks)
        filled = jnp.where(hit & (count == line), taken, filled)
        count = count + hit.astype(jnp.int32)
    table[1] = filled
    t_copy = pltpu.make_async_copy(table, stable, local_sem.at[2])
    t_copy.start()
    pv[listed_p] = jnp.zeros((block, block), jnp.bfloat16)
    kept[blocks] = jnp.zeros((block, block), jnp.bfloat16)
    t_copy.wait()

    def multiply(column):
        sides = []
        for r in range(rb):
            sides.append(jnp.concatenate(
                [pv[stable[0, r, column * listed_h + n]] for n in range(listed_h)], axis=1
            ))
        panel = hall[column].reshape(listed_h * block, block)
        product = jnp.dot(
            jnp.concatenate(sides, axis=0), panel, preferred_element_type=jnp.float32
        ).astype(jnp.bfloat16)
        for r in range(rb):
            kept[r * ncb + column] = product[r * block:(r + 1) * block]

    for step in range(1, cols):
        first_copy(step).wait_recv()
        for i in range(dims):
            plane_copy(step, 0, 2**i, flip(me_r, strides[i]), move_send, move_recv).start()
        core_copy(step, 0).start()
    p_copy.wait()
    h_copy.wait()
    multiply(me_c)
    for place in range(1, places):
        made = place.bit_length() - 1
        for step in range(1, cols):
            plane_copy(step, place, place, me_r, move_send, move_recv).wait_recv()
            for i in range(made + 1, dims):
                plane_copy(
                    step, place, 2**i + place, flip(me_r, strides[i]), move_send, move_recv
                ).start()
            core_copy(step, place).start()
    for step in range(1, cols):
        for place in range(places):
            other = flip(pieces[place], jnp.int32(1))
            pltpu.make_async_remote_copy(
                src_ref=hall.at[origin(step), other], dst_ref=hall.at[origin(step), other],
                send_sem=core_send.at[step, place], recv_sem=core_recv.at[step, place],
                device_id=(partner, me_c), device_id_type=MESH,
            ).wait_recv()
        multiply(origin(step))

    def deal(step):
        owner = xor(me_r, step)
        return pltpu.make_async_remote_copy(
            src_ref=outgoing.at[owner], dst_ref=out_ref.at[me_r],
            send_sem=deal_send.at[step], recv_sem=deal_recv.at[step],
            device_id=(owner, me_c), device_id_type=MESH,
        )

    for step in range(rows - 1, -1, -1):
        owner = xor(me_r, step)
        for s in range(SEND_CAP):
            outgoing[owner, s] = kept[stable[1, s, owner]]
        if step:
            deal(step).start()
    own = pltpu.make_async_copy(outgoing.at[me_r], out_ref.at[me_r], local_sem.at[3])
    own.start()
    for step in range(1, cols):
        first_copy(step).wait_send()
        for place in range(places):
            if place:
                plane_copy(step, 0, place, me_r, move_send, move_recv).wait_send()
            core_copy(step, place).wait_send()
    for step in range(rows - 1, 0, -1):
        deal(step).wait_send()
        deal(step).wait_recv()
    own.wait()


def local(rows, cols, p_blocks, p_positions, h_blocks, h_rows, keep_mask, owner_ids):
    listed_p, block = p_blocks.shape[:2]
    listed_h = h_blocks.shape[0]
    blocks = keep_mask.size
    depth = listed_h * block // rows
    places = rows // 2
    width = -(-max(h_rows.shape[0], rows) // LANES) * LANES
    smem = pl.BlockSpec(memory_space=pltpu.SMEM)
    anywhere = pl.BlockSpec(memory_space=pl.ANY)
    dma = pltpu.SemaphoreType.DMA
    return pl.pallas_call(
        functools.partial(kernel, rows, cols),
        out_shape=jax.ShapeDtypeStruct((rows, SEND_CAP, block, block), jnp.bfloat16),
        in_specs=[smem] * 4 + [anywhere] * 2,
        out_specs=anywhere,
        scratch_shapes=[
            pltpu.VMEM((listed_p + 1, block, block), jnp.bfloat16),
            pltpu.VMEM((cols, rows, depth, block), jnp.bfloat16),
            pltpu.VMEM((blocks + 1, block, block), jnp.bfloat16),
            pltpu.VMEM((rows, SEND_CAP, block, block), jnp.bfloat16),
            pltpu.VMEM((2, 8, width), jnp.int32),
            pltpu.SMEM((2, 8, width), jnp.int32),
            dma((4,)),
            dma((cols, places)),
            dma((cols, places)),
            dma((cols, places)),
            dma((cols, places)),
            dma((rows,)),
            dma((rows,)),
        ],
        compiler_params=pltpu.CompilerParams(
            collective_id=0, has_side_effects=True, vmem_limit_bytes=32 * 1024 * 1024
        ),
    )(
        p_positions, h_rows, keep_mask, owner_ids, p_blocks,
        h_blocks.reshape(rows, depth, block),
    )


def solution(mesh):
    return jax.shard_map(
        functools.partial(local, mesh.shape["row"], mesh.shape["col"]),
        mesh=mesh,
        in_specs=(
            P(("row", "col"), None, None),
            P(("row", "col")),
            P("col", None, None),
            P(),
            P(("row", "col"), None),
            P(("row", "col"), None, None),
        ),
        out_specs=P(("row", "col"), None, None, None),
        check_vma=False,
    )
```

```python
import functools

import jax
import jax.numpy as jnp
from jax import lax
from jax.experimental import pallas as pl
from jax.experimental.pallas import tpu as pltpu
from jax.sharding import PartitionSpec as P

KB = 64
SEND_CAP = 2
LANES = 128
UNROLL = 64
MESH = pl.DeviceIdType.MESH


def repeat(count, body, init=None):
    if count <= UNROLL:
        for i in range(count):
            init = body(i, init)
        return init
    return lax.fori_loop(0, count, body, init)


def xor(value, mask):
    bit = 1
    while bit <= mask:
        if mask & bit:
            value = value + bit * (1 - 2 * lax.rem(lax.div(value, bit), 2))
        bit *= 2
    return value


def kernel(
    rows, cols, pos_in, hrow_in, keep_in, owner_in, p_ref, h_ref, out_ref,
    pos_ref, hrow_ref, keep_ref, owner_ref, pv, hall, kept, outgoing, table, stable,
    local_sem, move_send, move_recv, core_send, core_recv, deal_send, deal_recv,
):
    me_r, me_c = lax.axis_index("row"), lax.axis_index("col")
    core = lax.rem(me_r, 2)
    listed_p = p_ref.shape[0]
    block = p_ref.shape[-1]
    rb, ncb = keep_ref.shape
    blocks = rb * ncb
    listed_h = hrow_ref.shape[0] // cols
    dims = rows.bit_length() - 2
    places = 2**dims
    power = cols & (cols - 1) == 0

    def target(step):
        return xor(me_c, step) if power else lax.rem(me_c + step, cols)

    def origin(step):
        return xor(me_c, step) if power else lax.rem(me_c + cols - step, cols)

    strides = []
    for i in range(dims):
        first, second = 2 ** (dims - i), 2 ** (i + 1)
        moves = [stride * (1 - 2 * lax.rem(lax.div(me_r, stride), 2)) for stride in (first, second)]
        strides.append(moves[0] + core * (moves[1] - moves[0]))
    pieces = [me_r]
    for stride in strides:
        pieces = pieces + [piece + stride for piece in pieces]
    toward = 1 - 2 * core
    partner = me_r + toward

    p_copy = pltpu.make_async_copy(p_ref, pv.at[pl.ds(0, listed_p)], local_sem.at[0])
    h_copy = pltpu.make_async_copy(h_ref, hall.at[me_c], local_sem.at[1])
    small = [
        pltpu.make_async_copy(given, held, local_sem.at[4 + i])
        for i, (given, held) in enumerate((
            (pos_in, pos_ref), (hrow_in, hrow_ref), (keep_in, keep_ref), (owner_in, owner_ref)
        ))
    ]
    for copy in small:
        copy.start()

    barrier = pltpu.get_barrier_semaphore()
    for step in range(1, cols):
        pl.semaphore_signal(barrier, inc=1, device_id=(me_r, target(step)), device_id_type=MESH)
    for step in range(1, rows):
        pl.semaphore_signal(barrier, inc=1, device_id=(xor(me_r, step), me_c), device_id_type=MESH)
    h_copy.start()
    p_copy.start()
    pl.semaphore_wait(barrier, cols + rows - 2)

    def first_copy(step):
        return pltpu.make_async_remote_copy(
            src_ref=h_ref.at[me_r], dst_ref=hall.at[me_c, me_r],
            send_sem=move_send.at[step, 0], recv_sem=move_recv.at[step, 0],
            device_id=(me_r, target(step)), device_id_type=MESH,
        )

    def plane_copy(step, place, onto, to_row, sends, recvs):
        piece = hall.at[origin(step), pieces[place]]
        return pltpu.make_async_remote_copy(
            src_ref=piece, dst_ref=piece,
            send_sem=sends.at[step, onto], recv_sem=recvs.at[step, onto],
            device_id=(to_row, me_c), device_id_type=MESH,
        )

    def core_copy(step, place):
        return plane_copy(step, place, place, partner, core_send, core_recv)

    for step in range(1, cols):
        first_copy(step).start()
    for copy in small:
        copy.wait()

    width = table.shape[-1]
    lane = lax.broadcasted_iota(jnp.int32, (8, width), 1)
    line = lax.broadcasted_iota(jnp.int32, (8, width), 0)
    wanted = repeat(
        hrow_ref.shape[0], lambda m, held: jnp.where(lane == m, hrow_ref[m], held),
        jnp.full((8, width), -1, jnp.int32),
    )
    wanted = jnp.where(wanted < 0, -1, wanted + line * KB)
    table[0] = repeat(
        listed_p, lambda q, held: jnp.where(wanted == pos_ref[q], q, held),
        jnp.full((8, width), listed_p, jnp.int32),
    )
    filled = jnp.full((8, width), blocks, jnp.int32)
    count = jnp.zeros((8, width), jnp.int32)
    for b in range(blocks):
        r, j = b // ncb, b % ncb
        hit = lane == owner_ref[r, 0, j]
        taken = jnp.where(keep_ref[r, j] == 1, b, blocks)
        filled = jnp.where(hit & (count == line), taken, filled)
        count = count + hit.astype(jnp.int32)
    table[1] = filled
    t_copy = pltpu.make_async_copy(table, stable, local_sem.at[2])
    t_copy.start()
    pv[listed_p] = jnp.zeros((block, block), jnp.bfloat16)
    kept[blocks] = jnp.zeros((block, block), jnp.bfloat16)
    t_copy.wait()

    def multiply(column):
        sides = []
        for r in range(rb):
            sides.append(jnp.concatenate(
                [pv[stable[0, r, column * listed_h + n]] for n in range(listed_h)], axis=1
            ))
        panel = hall[column].reshape(listed_h * block, block)
        product = jnp.dot(
            jnp.concatenate(sides, axis=0), panel, preferred_element_type=jnp.float32
        ).astype(jnp.bfloat16)
        for r in range(rb):
            kept[r * ncb + column] = product[r * block:(r + 1) * block]

    for step in range(1, cols):
        first_copy(step).wait_recv()
        for i in range(dims):
            plane_copy(step, 0, 2**i, me_r + strides[i], move_send, move_recv).start()
        core_copy(step, 0).start()
    p_copy.wait()
    h_copy.wait()
    multiply(me_c)
    for place in range(1, places):
        made = place.bit_length() - 1
        for step in range(1, cols):
            plane_copy(step, place, place, me_r, move_send, move_recv).wait_recv()
            for i in range(made + 1, dims):
                plane_copy(
                    step, place, 2**i + place, me_r + strides[i], move_send, move_recv
                ).start()
            core_copy(step, place).start()
    for step in range(1, cols):
        for place in range(places):
            other = pieces[place] + toward
            pltpu.make_async_remote_copy(
                src_ref=hall.at[origin(step), other], dst_ref=hall.at[origin(step), other],
                send_sem=core_send.at[step, place], recv_sem=core_recv.at[step, place],
                device_id=(partner, me_c), device_id_type=MESH,
            ).wait_recv()
        multiply(origin(step))

    def deal(step):
        owner = xor(me_r, step)
        return pltpu.make_async_remote_copy(
            src_ref=outgoing.at[owner], dst_ref=out_ref.at[me_r],
            send_sem=deal_send.at[step], recv_sem=deal_recv.at[step],
            device_id=(owner, me_c), device_id_type=MESH,
        )

    for step in range(rows - 1, -1, -1):
        owner = xor(me_r, step)
        for s in range(SEND_CAP):
            outgoing[owner, s] = kept[stable[1, s, owner]]
        if step:
            deal(step).start()
    own = pltpu.make_async_copy(outgoing.at[me_r], out_ref.at[me_r], local_sem.at[3])
    own.start()
    for step in range(1, cols):
        first_copy(step).wait_send()
        for place in range(places):
            if place:
                plane_copy(step, 0, place, me_r, move_send, move_recv).wait_send()
            core_copy(step, place).wait_send()
    for step in range(rows - 1, 0, -1):
        deal(step).wait_send()
        deal(step).wait_recv()
    own.wait()


def local(rows, cols, p_blocks, p_positions, h_blocks, h_rows, keep_mask, owner_ids):
    listed_p, block = p_blocks.shape[:2]
    listed_h = h_blocks.shape[0]
    blocks = keep_mask.size
    depth = listed_h * block // rows
    places = rows // 2
    width = -(-max(h_rows.shape[0], rows) // LANES) * LANES
    hbm = pl.BlockSpec(memory_space=pltpu.HBM)
    anywhere = pl.BlockSpec(memory_space=pl.ANY)
    dma = pltpu.SemaphoreType.DMA
    return pl.pallas_call(
        functools.partial(kernel, rows, cols),
        out_shape=jax.ShapeDtypeStruct((rows, SEND_CAP, block, block), jnp.bfloat16),
        in_specs=[hbm] * 6,
        out_specs=anywhere,
        scratch_shapes=[
            pltpu.SMEM(p_positions.shape, jnp.int32),
            pltpu.SMEM(h_rows.shape, jnp.int32),
            pltpu.SMEM(keep_mask.shape, jnp.int32),
            pltpu.SMEM((keep_mask.shape[0], 1, keep_mask.shape[1]), jnp.int32),
            pltpu.VMEM((listed_p + 1, block, block), jnp.bfloat16),
            pltpu.VMEM((cols, rows, depth, block), jnp.bfloat16),
            pltpu.VMEM((blocks + 1, block, block), jnp.bfloat16),
            pltpu.VMEM((rows, SEND_CAP, block, block), jnp.bfloat16),
            pltpu.VMEM((2, 8, width), jnp.int32),
            pltpu.SMEM((2, 8, width), jnp.int32),
            dma((8,)),
            dma((cols, places)),
            dma((cols, places)),
            dma((cols, places)),
            dma((cols, places)),
            dma((rows,)),
            dma((rows,)),
        ],
        compiler_params=pltpu.CompilerParams(
            collective_id=0, has_side_effects=True, vmem_limit_bytes=56 * 1024 * 1024
        ),
    )(
        p_positions, h_rows, keep_mask, jnp.transpose(owner_ids, (0, 2, 1)), p_blocks,
        h_blocks.reshape(rows, depth, block),
    )


def solution(mesh):
    return jax.shard_map(
        functools.partial(local, mesh.shape["row"], mesh.shape["col"]),
        mesh=mesh,
        in_specs=(
            P(("row", "col"), None, None),
            P(("row", "col")),
            P("col", None, None),
            P(),
            P(("row", "col"), None),
            P(("row", "col"), None, None),
        ),
        out_specs=P(("row", "col"), None, None, None),
        check_vma=False,
    )
```

```python
import functools

import jax
import jax.numpy as jnp
from jax import lax
from jax.experimental import pallas as pl
from jax.experimental.pallas import tpu as pltpu
from jax.sharding import PartitionSpec as P

KB = 64
SEND_CAP = 2
LANES = 128
UNROLL = 64
MESH = pl.DeviceIdType.MESH


def repeat(count, body, init=None):
    if count <= UNROLL:
        for i in range(count):
            init = body(i, init)
        return init
    return lax.fori_loop(0, count, body, init)


def xor(value, mask):
    bit = 1
    while bit <= mask:
        if mask & bit:
            value = value + bit * (1 - 2 * lax.rem(lax.div(value, bit), 2))
        bit *= 2
    return value


def kernel(
    rows, cols, pos_in, hrow_in, keep_in, owner_in, p_ref, h_ref, out_ref,
    pos_ref, hrow_ref, keep_ref, owner_ref, pv, hall, kept, outgoing, table, stable,
    local_sem, move_send, move_recv, core_send, core_recv, deal_send, deal_recv,
):
    me_r, me_c = lax.axis_index("row"), lax.axis_index("col")
    core = lax.rem(me_r, 2)
    listed_p = p_ref.shape[0]
    block = p_ref.shape[-1]
    rb, ncb = keep_ref.shape
    blocks = rb * ncb
    listed_h = hrow_ref.shape[0] // cols
    dims = rows.bit_length() - 2
    places = 2**dims
    power = cols & (cols - 1) == 0

    def target(step):
        return xor(me_c, step) if power else lax.rem(me_c + step, cols)

    def origin(step):
        return xor(me_c, step) if power else lax.rem(me_c + cols - step, cols)

    strides = []
    for i in range(dims):
        first, second = 2 ** (dims - i), 2 ** (i + 1)
        moves = [stride * (1 - 2 * lax.rem(lax.div(me_r, stride), 2)) for stride in (first, second)]
        strides.append(moves[0] + core * (moves[1] - moves[0]))
    pieces = [me_r]
    for stride in strides:
        pieces = pieces + [piece + stride for piece in pieces]
    toward = 1 - 2 * core
    partner = me_r + toward

    p_copy = pltpu.make_async_copy(p_ref, pv.at[pl.ds(0, listed_p)], local_sem.at[0])
    h_copy = pltpu.make_async_copy(h_ref, hall.at[me_c], local_sem.at[1])
    small = [
        pltpu.make_async_copy(given, held, local_sem.at[4 + i])
        for i, (given, held) in enumerate((
            (pos_in, pos_ref), (hrow_in, hrow_ref), (keep_in, keep_ref), (owner_in, owner_ref)
        ))
    ]
    for copy in small:
        copy.start()

    barrier = pltpu.get_barrier_semaphore()
    for step in range(1, cols):
        pl.semaphore_signal(barrier, inc=1, device_id=(me_r, target(step)), device_id_type=MESH)
    for step in range(1, rows):
        pl.semaphore_signal(barrier, inc=1, device_id=(xor(me_r, step), me_c), device_id_type=MESH)
    h_copy.start()
    p_copy.start()
    pl.semaphore_wait(barrier, cols + rows - 2)

    def first_copy(step):
        return pltpu.make_async_remote_copy(
            src_ref=h_ref.at[me_r], dst_ref=hall.at[me_c, me_r],
            send_sem=move_send.at[step, 0], recv_sem=move_recv.at[step, 0],
            device_id=(me_r, target(step)), device_id_type=MESH,
        )

    def plane_copy(step, place, onto, to_row, sends, recvs):
        piece = hall.at[origin(step), pieces[place]]
        return pltpu.make_async_remote_copy(
            src_ref=piece, dst_ref=piece,
            send_sem=sends.at[step, onto], recv_sem=recvs.at[step, onto],
            device_id=(to_row, me_c), device_id_type=MESH,
        )

    def core_copy(step, place):
        return plane_copy(step, place, place, partner, core_send, core_recv)

    for step in range(1, cols):
        first_copy(step).start()
    for copy in small:
        copy.wait()

    width = table.shape[-1]
    lane = lax.broadcasted_iota(jnp.int32, (8, width), 1)
    line = lax.broadcasted_iota(jnp.int32, (8, width), 0)
    wanted = repeat(
        hrow_ref.shape[0], lambda m, held: jnp.where(lane == m, hrow_ref[m], held),
        jnp.full((8, width), -1, jnp.int32),
    )
    wanted = jnp.where(wanted < 0, -1, wanted + line * KB)
    table[0] = repeat(
        listed_p, lambda q, held: jnp.where(wanted == pos_ref[q], q, held),
        jnp.full((8, width), listed_p, jnp.int32),
    )
    filled = jnp.full((8, width), blocks, jnp.int32)
    count = jnp.zeros((8, width), jnp.int32)
    for b in range(blocks):
        r, j = b // ncb, b % ncb
        hit = lane == owner_ref[r, 0, j]
        taken = jnp.where(keep_ref[r, j] == 1, b, blocks)
        filled = jnp.where(hit & (count == line), taken, filled)
        count = count + hit.astype(jnp.int32)
    table[1] = filled
    t_copy = pltpu.make_async_copy(table, stable, local_sem.at[2])
    t_copy.start()
    pv[listed_p] = jnp.zeros((block, block), jnp.bfloat16)
    kept[blocks] = jnp.zeros((block, block), jnp.bfloat16)
    t_copy.wait()

    def multiply(column):
        sides = []
        for r in range(rb):
            sides.append(jnp.concatenate(
                [pv[stable[0, r, column * listed_h + n]] for n in range(listed_h)], axis=1
            ))
        panel = hall[column].reshape(listed_h * block, block)
        product = jnp.dot(
            jnp.concatenate(sides, axis=0), panel, preferred_element_type=jnp.float32
        ).astype(jnp.bfloat16)
        for r in range(rb):
            kept[r * ncb + column] = product[r * block:(r + 1) * block]

    for step in range(1, cols):
        first_copy(step).wait_recv()
        for place in range(places - 1, 0, -1):
            plane_copy(step, 0, place, pieces[place], move_send, move_recv).start()
        core_copy(step, 0).start()
    p_copy.wait()
    h_copy.wait()
    multiply(me_c)
    for step in range(1, cols):
        for place in range(1, places):
            plane_copy(step, place, place, me_r, move_send, move_recv).wait_recv()
            core_copy(step, place).start()
    for step in range(1, cols):
        for place in range(places):
            other = pieces[place] + toward
            pltpu.make_async_remote_copy(
                src_ref=hall.at[origin(step), other], dst_ref=hall.at[origin(step), other],
                send_sem=core_send.at[step, place], recv_sem=core_recv.at[step, place],
                device_id=(partner, me_c), device_id_type=MESH,
            ).wait_recv()
        multiply(origin(step))

    def deal(step):
        owner = xor(me_r, step)
        return pltpu.make_async_remote_copy(
            src_ref=outgoing.at[owner], dst_ref=out_ref.at[me_r],
            send_sem=deal_send.at[step], recv_sem=deal_recv.at[step],
            device_id=(owner, me_c), device_id_type=MESH,
        )

    for step in range(rows - 1, -1, -1):
        owner = xor(me_r, step)
        for s in range(SEND_CAP):
            outgoing[owner, s] = kept[stable[1, s, owner]]
        if step:
            deal(step).start()
    own = pltpu.make_async_copy(outgoing.at[me_r], out_ref.at[me_r], local_sem.at[3])
    own.start()
    for step in range(1, cols):
        first_copy(step).wait_send()
        for place in range(places):
            if place:
                plane_copy(step, 0, place, me_r, move_send, move_recv).wait_send()
            core_copy(step, place).wait_send()
    for step in range(rows - 1, 0, -1):
        deal(step).wait_send()
        deal(step).wait_recv()
    own.wait()


def local(rows, cols, p_blocks, p_positions, h_blocks, h_rows, keep_mask, owner_ids):
    listed_p, block = p_blocks.shape[:2]
    listed_h = h_blocks.shape[0]
    blocks = keep_mask.size
    depth = listed_h * block // rows
    places = rows // 2
    width = -(-max(h_rows.shape[0], rows) // LANES) * LANES
    hbm = pl.BlockSpec(memory_space=pltpu.HBM)
    anywhere = pl.BlockSpec(memory_space=pl.ANY)
    dma = pltpu.SemaphoreType.DMA
    return pl.pallas_call(
        functools.partial(kernel, rows, cols),
        out_shape=pltpu.VMEM((rows, SEND_CAP, block, block), jnp.bfloat16),
        in_specs=[hbm] * 6,
        out_specs=anywhere,
        scratch_shapes=[
            pltpu.SMEM(p_positions.shape, jnp.int32),
            pltpu.SMEM(h_rows.shape, jnp.int32),
            pltpu.SMEM(keep_mask.shape, jnp.int32),
            pltpu.SMEM((keep_mask.shape[0], 1, keep_mask.shape[1]), jnp.int32),
            pltpu.VMEM((listed_p + 1, block, block), jnp.bfloat16),
            pltpu.VMEM((cols, rows, depth, block), jnp.bfloat16),
            pltpu.VMEM((blocks + 1, block, block), jnp.bfloat16),
            pltpu.VMEM((rows, SEND_CAP, block, block), jnp.bfloat16),
            pltpu.VMEM((2, 8, width), jnp.int32),
            pltpu.SMEM((2, 8, width), jnp.int32),
            dma((8,)),
            dma((cols, places)),
            dma((cols, places)),
            dma((cols, places)),
            dma((cols, places)),
            dma((rows,)),
            dma((rows,)),
        ],
        compiler_params=pltpu.CompilerParams(
            collective_id=0, has_side_effects=True, vmem_limit_bytes=40 * 1024 * 1024
        ),
    )(*[
        pltpu.with_memory_space_constraint(given, pltpu.HBM) for given in (
            p_positions, h_rows, keep_mask, jnp.transpose(owner_ids, (0, 2, 1)), p_blocks,
            h_blocks.reshape(rows, depth, block),
        )
    ])


def solution(mesh):
    return jax.shard_map(
        functools.partial(local, mesh.shape["row"], mesh.shape["col"]),
        mesh=mesh,
        in_specs=(
            P(("row", "col"), None, None),
            P(("row", "col")),
            P("col", None, None),
            P(),
            P(("row", "col"), None),
            P(("row", "col"), None, None),
        ),
        out_specs=P(("row", "col"), None, None, None),
        check_vma=False,
    )
```

```python
import functools

import jax
import jax.numpy as jnp
from jax import lax
from jax.experimental import pallas as pl
from jax.experimental.pallas import tpu as pltpu
from jax.sharding import PartitionSpec as P

KB = 64
SEND_CAP = 2
HALVES = 2
LANES = 128
UNROLL = 64
MESH = pl.DeviceIdType.MESH


def repeat(count, body, init=None):
    if count <= UNROLL:
        for i in range(count):
            init = body(i, init)
        return init
    return lax.fori_loop(0, count, body, init)


def xor(value, mask):
    bit = 1
    while bit <= mask:
        if mask & bit:
            value = value + bit * (1 - 2 * lax.rem(lax.div(value, bit), 2))
        bit *= 2
    return value


def kernel(
    rows, cols, pos_in, hrow_in, keep_in, owner_in, p_ref, h_ref, out_ref,
    pos_ref, hrow_ref, keep_ref, owner_ref, pv, hown, hall, kept, outgoing, received, table, stable,
    local_sem, move_send, move_recv, core_send, core_recv, deal_send, deal_recv,
):
    me_r, me_c = lax.axis_index("row"), lax.axis_index("col")
    core = lax.rem(me_r, 2)
    listed_p = p_ref.shape[0]
    block = p_ref.shape[-1]
    rb, ncb = keep_ref.shape
    blocks = rb * ncb
    listed_h = hrow_ref.shape[0] // cols
    dims = rows.bit_length() - 2
    places = 2**dims
    power = cols & (cols - 1) == 0

    def target(step):
        return xor(me_c, step) if power else lax.rem(me_c + step, cols)

    def origin(step):
        return xor(me_c, step) if power else lax.rem(me_c + cols - step, cols)

    strides = []
    for i in range(dims):
        first, second = 2 ** (dims - i), 2 ** (i + 1)
        moves = [stride * (1 - 2 * lax.rem(lax.div(me_r, stride), 2)) for stride in (first, second)]
        strides.append(moves[0] + core * (moves[1] - moves[0]))
    pieces = [me_r]
    for stride in strides:
        pieces = pieces + [piece + stride for piece in pieces]
    partner = me_r + 1 - 2 * core
    half = block // HALVES
    left = lax.broadcasted_iota(jnp.int32, (block, block), 1) < half

    def swapped(tile):
        return pltpu.roll(tile, half, 1)

    def wide(tile):
        return tile.astype(jnp.float32)

    p_copy = pltpu.make_async_copy(p_ref, pv.at[pl.ds(0, listed_p)], local_sem.at[0])
    h_copy = pltpu.make_async_copy(h_ref, hown, local_sem.at[1])
    small = [
        pltpu.make_async_copy(given, held, local_sem.at[4 + i])
        for i, (given, held) in enumerate((
            (pos_in, pos_ref), (hrow_in, hrow_ref), (keep_in, keep_ref), (owner_in, owner_ref)
        ))
    ]
    h_copy.start()
    for copy in small:
        copy.start()

    barrier = pltpu.get_barrier_semaphore()
    for step in range(1, cols):
        pl.semaphore_signal(barrier, inc=1, device_id=(me_r, target(step)), device_id_type=MESH)
    for step in range(1, rows):
        pl.semaphore_signal(barrier, inc=1, device_id=(xor(me_r, step), me_c), device_id_type=MESH)
    p_copy.start()

    h_copy.wait()
    pairs = listed_h // 2
    halves = ([], [])
    for t in range(pairs):
        a, b = wide(hown[t]), wide(hown[pairs + t])
        halves[0].append(jnp.where(left, a, swapped(b)).astype(jnp.bfloat16))
        halves[1].append(jnp.where(left, swapped(a), b).astype(jnp.bfloat16))
    for k in range(HALVES):
        hall[k, me_c] = jnp.concatenate(halves[k], axis=0).reshape(hall.shape[2:])
    pl.semaphore_wait(barrier, cols + rows - 2)

    def first_copy(k, step):
        piece = hall.at[k, me_c, lax.div(me_r, 2), core]
        return pltpu.make_async_remote_copy(
            src_ref=piece, dst_ref=piece,
            send_sem=move_send.at[k * cols + step, 0], recv_sem=move_recv.at[k * cols + step, 0],
            device_id=(me_r, target(step)), device_id_type=MESH,
        )

    def plane_copy(k, step, place, onto):
        piece = hall.at[k, origin(step), lax.div(pieces[place], 2), core]
        return pltpu.make_async_remote_copy(
            src_ref=piece, dst_ref=piece,
            send_sem=move_send.at[k * cols + step, onto],
            recv_sem=move_recv.at[k * cols + step, onto],
            device_id=(pieces[onto], me_c), device_id_type=MESH,
        )

    def core_copy(k, step, side):
        held = hall.at[k, origin(step), :, side]
        return pltpu.make_async_remote_copy(
            src_ref=held, dst_ref=held,
            send_sem=core_send.at[k * cols + step], recv_sem=core_recv.at[k * cols + step],
            device_id=(partner, me_c), device_id_type=MESH,
        )

    for k in range(HALVES):
        for step in range(1, cols):
            first_copy(k, step).start()
    for copy in small:
        copy.wait()

    width = table.shape[-1]
    lane = lax.broadcasted_iota(jnp.int32, (8, width), 1)
    line = lax.broadcasted_iota(jnp.int32, (8, width), 0)
    wanted = repeat(
        hrow_ref.shape[0], lambda m, held: jnp.where(lane == m, hrow_ref[m], held),
        jnp.full((8, width), -1, jnp.int32),
    )
    wanted = jnp.where(wanted < 0, -1, wanted + line * KB)
    table[0] = repeat(
        listed_p, lambda q, held: jnp.where(wanted == pos_ref[q], q, held),
        jnp.full((8, width), listed_p, jnp.int32),
    )
    filled = jnp.full((8, width), blocks, jnp.int32)
    count = jnp.zeros((8, width), jnp.int32)
    for b in range(blocks):
        r, j = b // ncb, b % ncb
        hit = lane == owner_ref[r, 0, j]
        taken = jnp.where(keep_ref[r, j] == 1, b, blocks)
        filled = jnp.where(hit & (count == line), taken, filled)
        count = count + hit.astype(jnp.int32)
    table[1] = filled
    t_copy = pltpu.make_async_copy(table, stable, local_sem.at[2])
    t_copy.start()
    pv[listed_p] = jnp.zeros((block, block), jnp.bfloat16)
    for k in range(HALVES):
        for s in range(SEND_CAP):
            kept[k, s, blocks] = jnp.zeros((block, block), jnp.bfloat16)
    t_copy.wait()

    def multiply(k, column):
        panel = hall[k, column].reshape(pairs * block, block)
        parts = []
        for first in (0, pairs):
            sides = []
            for r in range(rb):
                sides.append(jnp.concatenate(
                    [pv[stable[0, r, column * listed_h + first + n]] for n in range(pairs)], axis=1
                ))
            parts.append(jnp.dot(
                jnp.concatenate(sides, axis=0), panel, preferred_element_type=jnp.float32
            ))
        for r in range(rb):
            low, high = [part[r * block:(r + 1) * block] for part in parts]
            total = jnp.where(left, low, high)
            total = total + swapped(total)
            zero = jnp.zeros_like(total)
            kept[k, 0, r * ncb + column] = jnp.where(left, total, zero).astype(jnp.bfloat16)
            kept[k, 1, r * ncb + column] = jnp.where(left, zero, total).astype(jnp.bfloat16)

    def deal_copy(k, step):
        owner = xor(me_r, step)
        return pltpu.make_async_remote_copy(
            src_ref=outgoing.at[k, owner], dst_ref=received.at[k, me_r],
            send_sem=deal_send.at[k * rows + step], recv_sem=deal_recv.at[k * rows + step],
            device_id=(owner, me_c), device_id_type=MESH,
        )

    def deal(k):
        for step in range(rows - 1, -1, -1):
            owner = xor(me_r, step)
            tile = kept[k, 0, stable[1, 0, owner]] + kept[k, 1, stable[1, 1, owner]]
            if step:
                outgoing[k, owner] = tile
                deal_copy(k, step).start()
            else:
                received[k, me_r] = tile

    for k in range(HALVES):
        for step in range(1, cols):
            first_copy(k, step).wait_recv()
            for place in range(places - 1, 0, -1):
                plane_copy(k, step, 0, place).start()
    p_copy.wait()
    for k in range(HALVES):
        multiply(k, me_c)
    for k in range(HALVES):
        for step in range(1, cols):
            for place in range(1, places):
                plane_copy(k, step, place, place).wait_recv()
            core_copy(k, step, core).start()
        for step in range(1, cols):
            core_copy(k, step, 1 - core).wait_recv()
            multiply(k, origin(step))
        deal(k)

    for k in range(HALVES):
        for step in range(1, cols):
            first_copy(k, step).wait_send()
            for place in range(1, places):
                plane_copy(k, step, 0, place).wait_send()
            core_copy(k, step, core).wait_send()
    for step in range(rows):
        sender = xor(me_r, step)
        if step:
            for k in range(HALVES):
                deal_copy(k, step).wait_send()
                deal_copy(k, step).wait_recv()
        a, b = wide(received[0, sender]), wide(received[1, sender])
        out_ref[sender, 0] = jnp.where(left, a, swapped(b)).astype(jnp.bfloat16)
        out_ref[sender, 1] = jnp.where(left, swapped(a), b).astype(jnp.bfloat16)


def local(rows, cols, p_blocks, p_positions, h_blocks, h_rows, keep_mask, owner_ids):
    listed_p, block = p_blocks.shape[:2]
    listed_h = h_blocks.shape[0]
    blocks = keep_mask.size
    depth = listed_h * block // rows // HALVES
    places = rows // 2
    width = -(-max(h_rows.shape[0], rows) // LANES) * LANES
    hbm = pl.BlockSpec(memory_space=pltpu.HBM)
    dma = pltpu.SemaphoreType.DMA
    return pl.pallas_call(
        functools.partial(kernel, rows, cols),
        out_shape=pltpu.VMEM((rows, SEND_CAP, block, block), jnp.bfloat16),
        in_specs=[hbm] * 6,
        out_specs=pl.BlockSpec(memory_space=pltpu.VMEM),
        scratch_shapes=[
            pltpu.SMEM(p_positions.shape, jnp.int32),
            pltpu.SMEM(h_rows.shape, jnp.int32),
            pltpu.SMEM(keep_mask.shape, jnp.int32),
            pltpu.SMEM((keep_mask.shape[0], 1, keep_mask.shape[1]), jnp.int32),
            pltpu.VMEM((listed_p + 1, block, block), jnp.bfloat16),
            pltpu.VMEM(h_blocks.shape, jnp.bfloat16),
            pltpu.VMEM((HALVES, cols, rows // 2, 2, depth, block), jnp.bfloat16),
            pltpu.VMEM((HALVES, SEND_CAP, blocks + 1, block, block), jnp.bfloat16),
            pltpu.VMEM((HALVES, rows, block, block), jnp.bfloat16),
            pltpu.VMEM((HALVES, rows, block, block), jnp.bfloat16),
            pltpu.VMEM((2, 8, width), jnp.int32),
            pltpu.SMEM((2, 8, width), jnp.int32),
            dma((8,)),
            dma((HALVES * cols, places)),
            dma((HALVES * cols, places)),
            dma((HALVES * cols,)),
            dma((HALVES * cols,)),
            dma((HALVES * rows,)),
            dma((HALVES * rows,)),
        ],
        compiler_params=pltpu.CompilerParams(
            collective_id=0, has_side_effects=True, vmem_limit_bytes=40 * 1024 * 1024
        ),
    )(*[
        pltpu.with_memory_space_constraint(given, pltpu.HBM) for given in (
            p_positions, h_rows, keep_mask, jnp.transpose(owner_ids, (0, 2, 1)), p_blocks,
            h_blocks,
        )
    ])


def solution(mesh):
    return jax.shard_map(
        functools.partial(local, mesh.shape["row"], mesh.shape["col"]),
        mesh=mesh,
        in_specs=(
            P(("row", "col"), None, None),
            P(("row", "col")),
            P("col", None, None),
            P(),
            P(("row", "col"), None),
            P(("row", "col"), None, None),
        ),
        out_specs=P(("row", "col"), None, None, None),
        check_vma=False,
    )
```

```python
import functools

import jax
import jax.numpy as jnp
from jax import lax
from jax.experimental import pallas as pl
from jax.experimental.pallas import tpu as pltpu
from jax.sharding import PartitionSpec as P

KB = 64
SEND_CAP = 2
HALVES = 2
LANES = 128
UNROLL = 64
MESH = pl.DeviceIdType.MESH


def repeat(count, body, init=None):
    if count <= UNROLL:
        for i in range(count):
            init = body(i, init)
        return init
    return lax.fori_loop(0, count, body, init)


def xor(value, mask):
    bit = 1
    while bit <= mask:
        if mask & bit:
            value = value + bit * (1 - 2 * lax.rem(lax.div(value, bit), 2))
        bit *= 2
    return value


def kernel(
    rows, cols, pos_in, hrow_in, keep_in, owner_in, p_ref, h_ref, out_ref,
    pos_ref, hrow_ref, keep_ref, owner_ref, pv, hown, hall, kept, outgoing, received, table, stable,
    local_sem, first_send, first_recv, plane_send, plane_recv, core_send, core_recv, deal_send, deal_recv,
):
    me_r, me_c = lax.axis_index("row"), lax.axis_index("col")
    core = lax.rem(me_r, 2)
    listed_p = p_ref.shape[0]
    block = p_ref.shape[-1]
    rb, ncb = keep_ref.shape
    blocks = rb * ncb
    listed_h = hrow_ref.shape[0] // cols
    power = cols & (cols - 1) == 0

    def target(step):
        return xor(me_c, step) if power else lax.rem(me_c + step, cols)

    def origin(step):
        return xor(me_c, step) if power else lax.rem(me_c + cols - step, cols)

    sides = [lax.rem(lax.div(me_r, stride), 2) for stride in (rows // 2, 2)]
    ways = [stride * (1 - 2 * side) for stride, side in zip((rows // 2, 2), sides)]
    side = sides[0] + core * (sides[1] - sides[0])
    friend = me_r + ways[0] + core * (ways[1] - ways[0])
    partner = me_r + 1 - 2 * core
    half = block // HALVES
    left = lax.broadcasted_iota(jnp.int32, (block, block), 1) < half

    def swapped(tile):
        return pltpu.roll(tile, half, 1)

    def wide(tile):
        return tile.astype(jnp.float32)

    p_copy = pltpu.make_async_copy(p_ref, pv.at[pl.ds(0, listed_p)], local_sem.at[0])
    h_copy = pltpu.make_async_copy(h_ref, hown, local_sem.at[1])
    small = [
        pltpu.make_async_copy(given, held, local_sem.at[4 + i])
        for i, (given, held) in enumerate((
            (pos_in, pos_ref), (hrow_in, hrow_ref), (keep_in, keep_ref), (owner_in, owner_ref)
        ))
    ]
    h_copy.start()
    for copy in small:
        copy.start()

    barrier = pltpu.get_barrier_semaphore()
    for step in range(1, cols):
        pl.semaphore_signal(barrier, inc=1, device_id=(me_r, target(step)), device_id_type=MESH)
    for step in range(1, rows):
        pl.semaphore_signal(barrier, inc=1, device_id=(xor(me_r, step), me_c), device_id_type=MESH)
    p_copy.start()

    h_copy.wait()
    pairs = listed_h // 2
    halves = ([], [])
    for t in range(pairs):
        a, b = wide(hown[t]), wide(hown[pairs + t])
        halves[0].append(jnp.where(left, a, swapped(b)).astype(jnp.bfloat16))
        halves[1].append(jnp.where(left, swapped(a), b).astype(jnp.bfloat16))
    for k in range(HALVES):
        hall[k, me_c] = jnp.concatenate(halves[k], axis=0).reshape(hall.shape[2:])
    pl.semaphore_wait(barrier, cols + rows - 2)

    def first_copy(k, step):
        piece = hall.at[k, me_c, side, core]
        return pltpu.make_async_remote_copy(
            src_ref=piece, dst_ref=piece,
            send_sem=first_send.at[k * cols + step], recv_sem=first_recv.at[k * cols + step],
            device_id=(me_r, target(step)), device_id_type=MESH,
        )

    def plane_copy(k, step, part):
        piece = hall.at[k, origin(step), part, core]
        return pltpu.make_async_remote_copy(
            src_ref=piece, dst_ref=piece,
            send_sem=plane_send.at[k * cols + step], recv_sem=plane_recv.at[k * cols + step],
            device_id=(friend, me_c), device_id_type=MESH,
        )

    def core_copy(k, step, part):
        held = hall.at[k, origin(step), :, part]
        return pltpu.make_async_remote_copy(
            src_ref=held, dst_ref=held,
            send_sem=core_send.at[k * cols + step], recv_sem=core_recv.at[k * cols + step],
            device_id=(partner, me_c), device_id_type=MESH,
        )

    for k in range(HALVES):
        for step in range(1, cols):
            first_copy(k, step).start()
    for copy in small:
        copy.wait()

    width = table.shape[-1]
    lane = lax.broadcasted_iota(jnp.int32, (8, width), 1)
    line = lax.broadcasted_iota(jnp.int32, (8, width), 0)
    wanted = repeat(
        hrow_ref.shape[0], lambda m, held: jnp.where(lane == m, hrow_ref[m], held),
        jnp.full((8, width), -1, jnp.int32),
    )
    wanted = jnp.where(wanted < 0, -1, wanted + line * KB)
    table[0] = repeat(
        listed_p, lambda q, held: jnp.where(wanted == pos_ref[q], q, held),
        jnp.full((8, width), listed_p, jnp.int32),
    )
    filled = jnp.full((8, width), blocks, jnp.int32)
    count = jnp.zeros((8, width), jnp.int32)
    for b in range(blocks):
        r, j = b // ncb, b % ncb
        hit = lane == owner_ref[r, 0, j]
        taken = jnp.where(keep_ref[r, j] == 1, b, blocks)
        filled = jnp.where(hit & (count == line), taken, filled)
        count = count + hit.astype(jnp.int32)
    table[1] = filled
    t_copy = pltpu.make_async_copy(table, stable, local_sem.at[2])
    t_copy.start()
    pv[listed_p] = jnp.zeros((block, block), jnp.bfloat16)
    for k in range(HALVES):
        for s in range(SEND_CAP):
            kept[k, s, blocks] = jnp.zeros((block, block), jnp.bfloat16)
    t_copy.wait()

    def multiply(k, column):
        panel = hall[k, column].reshape(pairs * block, block)
        parts = []
        for first in (0, pairs):
            lines = []
            for r in range(rb):
                lines.append(jnp.concatenate(
                    [pv[stable[0, r, column * listed_h + first + n]] for n in range(pairs)], axis=1
                ))
            parts.append(jnp.dot(
                jnp.concatenate(lines, axis=0), panel, preferred_element_type=jnp.float32
            ))
        for r in range(rb):
            low, high = [part[r * block:(r + 1) * block] for part in parts]
            total = jnp.where(left, low, high)
            total = total + swapped(total)
            zero = jnp.zeros_like(total)
            kept[k, 0, r * ncb + column] = jnp.where(left, total, zero).astype(jnp.bfloat16)
            kept[k, 1, r * ncb + column] = jnp.where(left, zero, total).astype(jnp.bfloat16)

    def deal_copy(k, step):
        owner = xor(me_r, step)
        return pltpu.make_async_remote_copy(
            src_ref=outgoing.at[k, owner], dst_ref=received.at[k, me_r],
            send_sem=deal_send.at[k * rows + step], recv_sem=deal_recv.at[k * rows + step],
            device_id=(owner, me_c), device_id_type=MESH,
        )

    def deal(k):
        for step in range(rows - 1, -1, -1):
            owner = xor(me_r, step)
            tile = kept[k, 0, stable[1, 0, owner]] + kept[k, 1, stable[1, 1, owner]]
            if step:
                outgoing[k, owner] = tile
                deal_copy(k, step).start()
            else:
                received[k, me_r] = tile

    for k in range(HALVES):
        for step in range(1, cols):
            first_copy(k, step).wait_recv()
            plane_copy(k, step, side).start()
    p_copy.wait()
    for k in range(HALVES):
        multiply(k, me_c)
    for k in range(HALVES):
        for step in range(1, cols):
            plane_copy(k, step, 1 - side).wait_recv()
            core_copy(k, step, core).start()
        for step in range(1, cols):
            core_copy(k, step, 1 - core).wait_recv()
            multiply(k, origin(step))
        deal(k)

    for k in range(HALVES):
        for step in range(1, cols):
            first_copy(k, step).wait_send()
            plane_copy(k, step, side).wait_send()
            core_copy(k, step, core).wait_send()
    for step in range(rows):
        sender = xor(me_r, step)
        if step:
            for k in range(HALVES):
                deal_copy(k, step).wait_send()
                deal_copy(k, step).wait_recv()
        a, b = wide(received[0, sender]), wide(received[1, sender])
        out_ref[sender, 0] = jnp.where(left, a, swapped(b)).astype(jnp.bfloat16)
        out_ref[sender, 1] = jnp.where(left, swapped(a), b).astype(jnp.bfloat16)


def local(rows, cols, p_blocks, p_positions, h_blocks, h_rows, keep_mask, owner_ids):
    listed_p, block = p_blocks.shape[:2]
    listed_h = h_blocks.shape[0]
    blocks = keep_mask.size
    depth = listed_h * block // HALVES // 4
    width = -(-max(h_rows.shape[0], rows) // LANES) * LANES
    hbm = pl.BlockSpec(memory_space=pltpu.HBM)
    dma = pltpu.SemaphoreType.DMA
    return pl.pallas_call(
        functools.partial(kernel, rows, cols),
        out_shape=pltpu.VMEM((rows, SEND_CAP, block, block), jnp.bfloat16),
        in_specs=[hbm] * 6,
        out_specs=pl.BlockSpec(memory_space=pltpu.VMEM),
        scratch_shapes=[
            pltpu.SMEM(p_positions.shape, jnp.int32),
            pltpu.SMEM(h_rows.shape, jnp.int32),
            pltpu.SMEM(keep_mask.shape, jnp.int32),
            pltpu.SMEM((keep_mask.shape[0], 1, keep_mask.shape[1]), jnp.int32),
            pltpu.VMEM((listed_p + 1, block, block), jnp.bfloat16),
            pltpu.VMEM(h_blocks.shape, jnp.bfloat16),
            pltpu.VMEM((HALVES, cols, 2, 2, depth, block), jnp.bfloat16),
            pltpu.VMEM((HALVES, SEND_CAP, blocks + 1, block, block), jnp.bfloat16),
            pltpu.VMEM((HALVES, rows, block, block), jnp.bfloat16),
            pltpu.VMEM((HALVES, rows, block, block), jnp.bfloat16),
            pltpu.VMEM((2, 8, width), jnp.int32),
            pltpu.SMEM((2, 8, width), jnp.int32),
            dma((8,)),
            dma((HALVES * cols,)),
            dma((HALVES * cols,)),
            dma((HALVES * cols,)),
            dma((HALVES * cols,)),
            dma((HALVES * cols,)),
            dma((HALVES * cols,)),
            dma((HALVES * rows,)),
            dma((HALVES * rows,)),
        ],
        compiler_params=pltpu.CompilerParams(
            collective_id=0, has_side_effects=True, vmem_limit_bytes=40 * 1024 * 1024
        ),
    )(*[
        pltpu.with_memory_space_constraint(given, pltpu.HBM) for given in (
            p_positions, h_rows, keep_mask, jnp.transpose(owner_ids, (0, 2, 1)), p_blocks,
            h_blocks,
        )
    ])


def solution(mesh):
    return jax.shard_map(
        functools.partial(local, mesh.shape["row"], mesh.shape["col"]),
        mesh=mesh,
        in_specs=(
            P(("row", "col"), None, None),
            P(("row", "col")),
            P("col", None, None),
            P(),
            P(("row", "col"), None),
            P(("row", "col"), None, None),
        ),
        out_specs=P(("row", "col"), None, None, None),
        check_vma=False,
    )
```

```python
import functools

import jax
import jax.numpy as jnp
from jax import lax
from jax.experimental import pallas as pl
from jax.experimental.pallas import tpu as pltpu
from jax.sharding import PartitionSpec as P

KB = 64
SEND_CAP = 2
LANES = 128
UNROLL = 64
MESH = pl.DeviceIdType.MESH


def repeat(count, body, init=None):
    if count <= UNROLL:
        for i in range(count):
            init = body(i, init)
        return init
    return lax.fori_loop(0, count, body, init)


def xor(value, mask):
    bit = 1
    while bit <= mask:
        if mask & bit:
            value = value + bit * (1 - 2 * lax.rem(lax.div(value, bit), 2))
        bit *= 2
    return value


def kernel(
    rows, cols, pos_in, hrow_in, keep_in, owner_in, p_ref, h_ref, out_ref,
    pos_ref, hrow_ref, keep_ref, owner_ref, pv, hall, kept, outgoing, table, stable,
    local_sem, move_send, move_recv, core_send, core_recv, deal_send, deal_recv,
):
    me_r, me_c = lax.axis_index("row"), lax.axis_index("col")
    core = lax.rem(me_r, 2)
    listed_p = p_ref.shape[0]
    block = p_ref.shape[-1]
    rb, ncb = keep_ref.shape
    blocks = rb * ncb
    listed_h = hrow_ref.shape[0] // cols
    dims = rows.bit_length() - 2
    places = 2**dims
    power = cols & (cols - 1) == 0

    def target(step):
        return xor(me_c, step) if power else lax.rem(me_c + step, cols)

    def origin(step):
        return xor(me_c, step) if power else lax.rem(me_c + cols - step, cols)

    strides = []
    for i in range(dims):
        first, second = 2 ** (dims - i), 2 ** (i + 1)
        moves = [stride * (1 - 2 * lax.rem(lax.div(me_r, stride), 2)) for stride in (first, second)]
        strides.append(moves[0] + core * (moves[1] - moves[0]))
    pieces = [me_r]
    for stride in strides:
        pieces = pieces + [piece + stride for piece in pieces]
    toward = 1 - 2 * core
    partner = me_r + toward

    barrier = pltpu.get_barrier_semaphore()
    for step in range(1, cols):
        pl.semaphore_signal(barrier, inc=1, device_id=(me_r, target(step)), device_id_type=MESH)
    for step in range(1, rows):
        pl.semaphore_signal(barrier, inc=1, device_id=(xor(me_r, step), me_c), device_id_type=MESH)

    p_copy = pltpu.make_async_copy(p_ref, pv.at[pl.ds(0, listed_p)], local_sem.at[0])
    h_copy = pltpu.make_async_copy(h_ref, hall.at[me_c], local_sem.at[1])
    small = [
        pltpu.make_async_copy(given, held, local_sem.at[4 + i])
        for i, (given, held) in enumerate((
            (pos_in, pos_ref), (hrow_in, hrow_ref), (keep_in, keep_ref), (owner_in, owner_ref)
        ))
    ]
    for copy in small:
        copy.start()
    h_copy.start()
    p_copy.start()
    pl.semaphore_wait(barrier, cols + rows - 2)

    def first_copy(step):
        return pltpu.make_async_remote_copy(
            src_ref=h_ref.at[lax.div(me_r, 2), core], dst_ref=hall.at[me_c, lax.div(me_r, 2), core],
            send_sem=move_send.at[step, 0], recv_sem=move_recv.at[step, 0],
            device_id=(me_r, target(step)), device_id_type=MESH,
        )

    def plane_copy(step, place, onto, to_row, sends, recvs):
        piece = hall.at[origin(step), lax.div(pieces[place], 2), core]
        return pltpu.make_async_remote_copy(
            src_ref=piece, dst_ref=piece,
            send_sem=sends.at[step, onto], recv_sem=recvs.at[step, onto],
            device_id=(to_row, me_c), device_id_type=MESH,
        )

    def core_copy(step, side):
        held = hall.at[origin(step), :, side]
        return pltpu.make_async_remote_copy(
            src_ref=held, dst_ref=held,
            send_sem=core_send.at[step], recv_sem=core_recv.at[step],
            device_id=(partner, me_c), device_id_type=MESH,
        )

    for step in range(1, cols):
        first_copy(step).start()
    for copy in small:
        copy.wait()

    width = table.shape[-1]
    lane = lax.broadcasted_iota(jnp.int32, (8, width), 1)
    line = lax.broadcasted_iota(jnp.int32, (8, width), 0)
    wanted = repeat(
        hrow_ref.shape[0], lambda m, held: jnp.where(lane == m, hrow_ref[m], held),
        jnp.full((8, width), -1, jnp.int32),
    )
    wanted = jnp.where(wanted < 0, -1, wanted + line * KB)
    found = repeat(
        listed_p, lambda q, held: jnp.where(wanted == pos_ref[q], q, held),
        jnp.full((8, width), listed_p, jnp.int32),
    )
    filled = jnp.full((8, width), blocks, jnp.int32)
    count = jnp.zeros((8, width), jnp.int32) + rb
    for b in range(blocks):
        r, j = b // ncb, b % ncb
        hit = lane == owner_ref[r, 0, j]
        taken = jnp.where(keep_ref[r, j] == 1, b, blocks)
        filled = jnp.where(hit & (count == line), taken, filled)
        count = count + hit.astype(jnp.int32)
    table[...] = jnp.where(line < rb, found, filled)
    t_copy = pltpu.make_async_copy(table, stable, local_sem.at[2])
    t_copy.start()
    pv[listed_p] = jnp.zeros((block, block), jnp.bfloat16)
    kept[blocks] = jnp.zeros((block, block), jnp.bfloat16)

    def multiply(column):
        sides = []
        for r in range(rb):
            sides.append(jnp.concatenate(
                [pv[stable[r, column * listed_h + n]] for n in range(listed_h)], axis=1
            ))
        panel = hall[column].reshape(listed_h * block, block)
        product = jnp.dot(
            jnp.concatenate(sides, axis=0), panel, preferred_element_type=jnp.float32
        ).astype(jnp.bfloat16)
        for r in range(rb):
            kept[r * ncb + column] = product[r * block:(r + 1) * block]

    for step in range(1, cols):
        first_copy(step).wait_recv()
        for place in range(places - 1, 0, -1):
            plane_copy(step, 0, place, pieces[place], move_send, move_recv).start()
    t_copy.wait()
    p_copy.wait()
    h_copy.wait()
    multiply(me_c)
    for step in range(1, cols + 2):
        if step < cols:
            for place in range(1, places):
                plane_copy(step, place, place, me_r, move_send, move_recv).wait_recv()
            core_copy(step, core).start()
        if step > 2:
            core_copy(step - 2, 1 - core).wait_recv()
            multiply(origin(step - 2))

    def deal(step):
        owner = xor(me_r, step)
        return pltpu.make_async_remote_copy(
            src_ref=outgoing.at[owner], dst_ref=out_ref.at[me_r],
            send_sem=deal_send.at[step], recv_sem=deal_recv.at[step],
            device_id=(owner, me_c), device_id_type=MESH,
        )

    for step in range(rows - 1, -1, -1):
        owner = xor(me_r, step)
        for s in range(SEND_CAP):
            outgoing[owner, s] = kept[stable[rb + s, owner]]
        if step:
            deal(step).start()
    own = pltpu.make_async_copy(outgoing.at[me_r], out_ref.at[me_r], local_sem.at[3])
    own.start()
    for step in range(1, cols):
        first_copy(step).wait_send()
        for place in range(1, places):
            plane_copy(step, 0, place, me_r, move_send, move_recv).wait_send()
        core_copy(step, core).wait_send()
    for step in range(rows - 1, 0, -1):
        deal(step).wait_send()
        deal(step).wait_recv()
    own.wait()


def local(rows, cols, p_blocks, p_positions, h_blocks, h_rows, keep_mask, owner_ids):
    listed_p, block = p_blocks.shape[:2]
    listed_h = h_blocks.shape[0]
    blocks = keep_mask.size
    depth = listed_h * block // rows
    places = rows // 2
    width = -(-max(h_rows.shape[0], rows) // LANES) * LANES
    hbm = pl.BlockSpec(memory_space=pltpu.HBM)
    anywhere = pl.BlockSpec(memory_space=pl.ANY)
    dma = pltpu.SemaphoreType.DMA
    return pl.pallas_call(
        functools.partial(kernel, rows, cols),
        out_shape=pltpu.VMEM((rows, SEND_CAP, block, block), jnp.bfloat16),
        in_specs=[hbm] * 6,
        out_specs=anywhere,
        scratch_shapes=[
            pltpu.SMEM(p_positions.shape, jnp.int32),
            pltpu.SMEM(h_rows.shape, jnp.int32),
            pltpu.SMEM(keep_mask.shape, jnp.int32),
            pltpu.SMEM((keep_mask.shape[0], 1, keep_mask.shape[1]), jnp.int32),
            pltpu.VMEM((listed_p + 1, block, block), jnp.bfloat16),
            pltpu.VMEM((cols, rows // 2, 2, depth, block), jnp.bfloat16),
            pltpu.VMEM((blocks + 1, block, block), jnp.bfloat16),
            pltpu.VMEM((rows, SEND_CAP, block, block), jnp.bfloat16),
            pltpu.VMEM((8, width), jnp.int32),
            pltpu.SMEM((8, width), jnp.int32),
            dma((8,)),
            dma((cols, places)),
            dma((cols, places)),
            dma((cols,)),
            dma((cols,)),
            dma((rows,)),
            dma((rows,)),
        ],
        compiler_params=pltpu.CompilerParams(
            collective_id=0, has_side_effects=True, vmem_limit_bytes=40 * 1024 * 1024
        ),
    )(*[
        pltpu.with_memory_space_constraint(given, pltpu.HBM) for given in (
            p_positions, h_rows, keep_mask, jnp.transpose(owner_ids, (0, 2, 1)), p_blocks,
            h_blocks.reshape(rows // 2, 2, depth, block),
        )
    ])


def solution(mesh):
    return jax.shard_map(
        functools.partial(local, mesh.shape["row"], mesh.shape["col"]),
        mesh=mesh,
        in_specs=(
            P(("row", "col"), None, None),
            P(("row", "col")),
            P("col", None, None),
            P(),
            P(("row", "col"), None),
            P(("row", "col"), None, None),
        ),
        out_specs=P(("row", "col"), None, None, None),
        check_vma=False,
    )
```

```python
import functools

import jax
import jax.numpy as jnp
from jax import lax
from jax.experimental import pallas as pl
from jax.experimental.pallas import tpu as pltpu
from jax.sharding import PartitionSpec as P

KB = 64
SEND_CAP = 2
LANES = 128
UNROLL = 64
MESH = pl.DeviceIdType.MESH


def repeat(count, body, init=None):
    if count <= UNROLL:
        for i in range(count):
            init = body(i, init)
        return init
    return lax.fori_loop(0, count, body, init)


def xor(value, mask):
    bit = 1
    while bit <= mask:
        if mask & bit:
            value = value + bit * (1 - 2 * lax.rem(lax.div(value, bit), 2))
        bit *= 2
    return value


def kernel(
    rows, cols, pos_in, hrow_in, keep_in, owner_in, p_ref, h_ref, out_ref,
    pos_ref, hrow_ref, keep_ref, owner_ref, pv, hall, kept, outgoing, table, stable,
    local_sem, first_send, move_send, move_recv, core_send, core_recv, deal_send, deal_recv,
):
    me_r, me_c = lax.axis_index("row"), lax.axis_index("col")
    core = lax.rem(me_r, 2)
    listed_p = p_ref.shape[0]
    block = p_ref.shape[-1]
    rb, ncb = keep_ref.shape
    blocks = rb * ncb
    listed_h = hrow_ref.shape[0] // cols
    dims = rows.bit_length() - 2
    places = 2**dims
    before, after = me_c > 0, me_c < cols - 1
    near = jnp.minimum(me_c, cols - 1 - me_c)
    far_way = jnp.where(me_c > cols - 1 - me_c, -1, 1)
    origins = [me_c]
    for step in range(1, cols):
        close = (step + 1) // 2 * (1 if step % 2 else -1)
        origins.append(me_c + jnp.where(step <= 2 * near, close, far_way * (step - near)))

    strides = []
    for i in range(dims):
        first, second = 2 ** (dims - i), 2 ** (i + 1)
        moves = [stride * (1 - 2 * lax.rem(lax.div(me_r, stride), 2)) for stride in (first, second)]
        strides.append(moves[0] + core * (moves[1] - moves[0]))
    pieces = [me_r]
    for stride in strides:
        pieces = pieces + [piece + stride for piece in pieces]
    toward = 1 - 2 * core
    partner = me_r + toward

    barrier = pltpu.get_barrier_semaphore()
    for exists, way in ((before, -1), (after, 1)):
        @pl.when(exists)
        def _():
            pl.semaphore_signal(barrier, inc=1, device_id=(me_r, me_c + way), device_id_type=MESH)

    for step in range(1, rows):
        pl.semaphore_signal(barrier, inc=1, device_id=(xor(me_r, step), me_c), device_id_type=MESH)

    p_copy = pltpu.make_async_copy(p_ref, pv.at[pl.ds(0, listed_p)], local_sem.at[0])
    h_copy = pltpu.make_async_copy(h_ref, hall.at[me_c], local_sem.at[1])
    small = [
        pltpu.make_async_copy(given, held, local_sem.at[4 + i])
        for i, (given, held) in enumerate((
            (pos_in, pos_ref), (hrow_in, hrow_ref), (keep_in, keep_ref), (owner_in, owner_ref)
        ))
    ]
    for copy in small:
        copy.start()
    h_copy.start()
    p_copy.start()
    pl.semaphore_wait(barrier, rows - 1 + jnp.minimum(me_c, 1) + jnp.minimum(cols - 1 - me_c, 1))

    def first_copy(way):
        return pltpu.make_async_remote_copy(
            src_ref=h_ref.at[lax.div(me_r, 2), core], dst_ref=hall.at[me_c, lax.div(me_r, 2), core],
            send_sem=first_send.at[(way + 1) // 2], recv_sem=move_recv.at[me_c, 0],
            device_id=(me_r, me_c + way), device_id_type=MESH,
        )

    def relay_copy(step):
        from_panel = origins[step]
        piece = hall.at[from_panel, lax.div(me_r, 2), core]
        return pltpu.make_async_remote_copy(
            src_ref=piece, dst_ref=piece,
            send_sem=move_send.at[from_panel, 0], recv_sem=move_recv.at[from_panel, 0],
            device_id=(me_r, me_c + jnp.where(from_panel < me_c, 1, -1)), device_id_type=MESH,
        )

    def passes(step):
        return ((origins[step] < me_c) & after) | ((origins[step] > me_c) & before)

    def plane_copy(step, place, onto, to_row, sends, recvs):
        piece = hall.at[origins[step], lax.div(pieces[place], 2), core]
        return pltpu.make_async_remote_copy(
            src_ref=piece, dst_ref=piece,
            send_sem=sends.at[origins[step], onto], recv_sem=recvs.at[origins[step], onto],
            device_id=(to_row, me_c), device_id_type=MESH,
        )

    def core_copy(step, side):
        held = hall.at[origins[step], :, side]
        return pltpu.make_async_remote_copy(
            src_ref=held, dst_ref=held,
            send_sem=core_send.at[origins[step]], recv_sem=core_recv.at[origins[step]],
            device_id=(partner, me_c), device_id_type=MESH,
        )

    for exists, way in ((before, -1), (after, 1)):
        @pl.when(exists)
        def _():
            first_copy(way).start()

    for copy in small:
        copy.wait()

    width = table.shape[-1]
    lane = lax.broadcasted_iota(jnp.int32, (8, width), 1)
    line = lax.broadcasted_iota(jnp.int32, (8, width), 0)
    wanted = repeat(
        hrow_ref.shape[0], lambda m, held: jnp.where(lane == m, hrow_ref[m], held),
        jnp.full((8, width), -1, jnp.int32),
    )
    wanted = jnp.where(wanted < 0, -1, wanted + line * KB)
    found = repeat(
        listed_p, lambda q, held: jnp.where(wanted == pos_ref[q], q, held),
        jnp.full((8, width), listed_p, jnp.int32),
    )
    filled = jnp.full((8, width), blocks, jnp.int32)
    count = jnp.zeros((8, width), jnp.int32) + rb
    for b in range(blocks):
        r, j = b // ncb, b % ncb
        hit = lane == owner_ref[r, 0, j]
        taken = jnp.where(keep_ref[r, j] == 1, b, blocks)
        filled = jnp.where(hit & (count == line), taken, filled)
        count = count + hit.astype(jnp.int32)
    table[...] = jnp.where(line < rb, found, filled)
    t_copy = pltpu.make_async_copy(table, stable, local_sem.at[2])
    t_copy.start()
    pv[listed_p] = jnp.zeros((block, block), jnp.bfloat16)
    kept[blocks] = jnp.zeros((block, block), jnp.bfloat16)

    def multiply(column):
        sides = []
        for r in range(rb):
            sides.append(jnp.concatenate(
                [pv[stable[r, column * listed_h + n]] for n in range(listed_h)], axis=1
            ))
        panel = hall[column].reshape(listed_h * block, block)
        product = jnp.dot(
            jnp.concatenate(sides, axis=0), panel, preferred_element_type=jnp.float32
        ).astype(jnp.bfloat16)
        for r in range(rb):
            kept[r * ncb + column] = product[r * block:(r + 1) * block]

    for step in range(1, cols):
        relay_copy(step).wait_recv()

        @pl.when(passes(step))
        def _():
            relay_copy(step).start()

        for place in range(places - 1, 0, -1):
            plane_copy(step, 0, place, pieces[place], move_send, move_recv).start()
    t_copy.wait()
    p_copy.wait()
    h_copy.wait()
    multiply(me_c)
    for step in range(1, cols + 2):
        if step < cols:
            for place in range(1, places):
                plane_copy(step, place, place, me_r, move_send, move_recv).wait_recv()
            core_copy(step, core).start()
        if step > 2:
            core_copy(step - 2, 1 - core).wait_recv()
            multiply(origins[step - 2])

    def deal(step):
        owner = xor(me_r, step)
        return pltpu.make_async_remote_copy(
            src_ref=outgoing.at[owner], dst_ref=out_ref.at[me_r],
            send_sem=deal_send.at[step], recv_sem=deal_recv.at[step],
            device_id=(owner, me_c), device_id_type=MESH,
        )

    for step in range(rows - 1, -1, -1):
        owner = xor(me_r, step)
        for s in range(SEND_CAP):
            outgoing[owner, s] = kept[stable[rb + s, owner]]
        if step:
            deal(step).start()
    own = pltpu.make_async_copy(outgoing.at[me_r], out_ref.at[me_r], local_sem.at[3])
    own.start()
    for exists, way in ((before, -1), (after, 1)):
        @pl.when(exists)
        def _():
            first_copy(way).wait_send()

    for step in range(1, cols):
        @pl.when(passes(step))
        def _():
            relay_copy(step).wait_send()

        for place in range(1, places):
            plane_copy(step, 0, place, me_r, move_send, move_recv).wait_send()
        core_copy(step, core).wait_send()
    for step in range(rows - 1, 0, -1):
        deal(step).wait_send()
        deal(step).wait_recv()
    own.wait()


def local(rows, cols, p_blocks, p_positions, h_blocks, h_rows, keep_mask, owner_ids):
    listed_p, block = p_blocks.shape[:2]
    listed_h = h_blocks.shape[0]
    blocks = keep_mask.size
    depth = listed_h * block // rows
    places = rows // 2
    width = -(-max(h_rows.shape[0], rows) // LANES) * LANES
    hbm = pl.BlockSpec(memory_space=pltpu.HBM)
    anywhere = pl.BlockSpec(memory_space=pl.ANY)
    dma = pltpu.SemaphoreType.DMA
    return pl.pallas_call(
        functools.partial(kernel, rows, cols),
        out_shape=pltpu.VMEM((rows, SEND_CAP, block, block), jnp.bfloat16),
        in_specs=[hbm] * 6,
        out_specs=anywhere,
        scratch_shapes=[
            pltpu.SMEM(p_positions.shape, jnp.int32),
            pltpu.SMEM(h_rows.shape, jnp.int32),
            pltpu.SMEM(keep_mask.shape, jnp.int32),
            pltpu.SMEM((keep_mask.shape[0], 1, keep_mask.shape[1]), jnp.int32),
            pltpu.VMEM((listed_p + 1, block, block), jnp.bfloat16),
            pltpu.VMEM((cols, rows // 2, 2, depth, block), jnp.bfloat16),
            pltpu.VMEM((blocks + 1, block, block), jnp.bfloat16),
            pltpu.VMEM((rows, SEND_CAP, block, block), jnp.bfloat16),
            pltpu.VMEM((8, width), jnp.int32),
            pltpu.SMEM((8, width), jnp.int32),
            dma((8,)),
            dma((2,)),
            dma((cols, places)),
            dma((cols, places)),
            dma((cols,)),
            dma((cols,)),
            dma((rows,)),
            dma((rows,)),
        ],
        compiler_params=pltpu.CompilerParams(
            collective_id=0, has_side_effects=True, vmem_limit_bytes=40 * 1024 * 1024
        ),
    )(*[
        pltpu.with_memory_space_constraint(given, pltpu.HBM) for given in (
            p_positions, h_rows, keep_mask, jnp.transpose(owner_ids, (0, 2, 1)), p_blocks,
            h_blocks.reshape(rows // 2, 2, depth, block),
        )
    ])


def solution(mesh):
    return jax.shard_map(
        functools.partial(local, mesh.shape["row"], mesh.shape["col"]),
        mesh=mesh,
        in_specs=(
            P(("row", "col"), None, None),
            P(("row", "col")),
            P("col", None, None),
            P(),
            P(("row", "col"), None),
            P(("row", "col"), None, None),
        ),
        out_specs=P(("row", "col"), None, None, None),
        check_vma=False,
    )
```

```python
import functools

import jax
import jax.numpy as jnp
from jax import lax
from jax.experimental import pallas as pl
from jax.experimental.pallas import tpu as pltpu
from jax.sharding import PartitionSpec as P

KB = 64
SEND_CAP = 2
HALVES = 2
LANES = 128
UNROLL = 64
MESH = pl.DeviceIdType.MESH


def repeat(count, body, init=None):
    if count <= UNROLL:
        for i in range(count):
            init = body(i, init)
        return init
    return lax.fori_loop(0, count, body, init)


def xor(value, mask):
    bit = 1
    while bit <= mask:
        if mask & bit:
            value = value + bit * (1 - 2 * lax.rem(lax.div(value, bit), 2))
        bit *= 2
    return value


def kernel(
    rows, cols, pos_in, hrow_in, keep_in, owner_in, p_ref, h_ref, out_ref,
    pos_ref, hrow_ref, keep_ref, owner_ref, pv, hown, hall, kept, outgoing, received, table, stable,
    local_sem, move_send, move_recv, core_send, core_recv, deal_send, deal_recv,
):
    me_r, me_c = lax.axis_index("row"), lax.axis_index("col")
    core = lax.rem(me_r, 2)
    listed_p = p_ref.shape[0]
    block = p_ref.shape[-1]
    rb, ncb = keep_ref.shape
    blocks = rb * ncb
    listed_h = hrow_ref.shape[0] // cols
    dims = rows.bit_length() - 2
    places = 2**dims
    power = cols & (cols - 1) == 0

    def target(step):
        return xor(me_c, step) if power else lax.rem(me_c + step, cols)

    def origin(step):
        return xor(me_c, step) if power else lax.rem(me_c + cols - step, cols)

    strides = []
    for i in range(dims):
        first, second = 2 ** (dims - i), 2 ** (i + 1)
        moves = [stride * (1 - 2 * lax.rem(lax.div(me_r, stride), 2)) for stride in (first, second)]
        strides.append(moves[0] + core * (moves[1] - moves[0]))
    pieces = [me_r]
    for stride in strides:
        pieces = pieces + [piece + stride for piece in pieces]
    partner = me_r + 1 - 2 * core
    barrier = pltpu.get_barrier_semaphore()
    for step in range(1, cols):
        pl.semaphore_signal(barrier, inc=1, device_id=(me_r, target(step)), device_id_type=MESH)
    for step in range(1, rows):
        pl.semaphore_signal(barrier, inc=1, device_id=(xor(me_r, step), me_c), device_id_type=MESH)

    half = block // HALVES
    left = lax.broadcasted_iota(jnp.int32, (block, block), 1) < half

    def swapped(tile):
        return pltpu.roll(tile, half, 1)

    def wide(tile):
        return tile.astype(jnp.float32)

    p_copy = pltpu.make_async_copy(p_ref, pv.at[pl.ds(0, listed_p)], local_sem.at[0])
    h_copy = pltpu.make_async_copy(h_ref, hown, local_sem.at[1])
    small = [
        pltpu.make_async_copy(given, held, local_sem.at[4 + i])
        for i, (given, held) in enumerate((
            (pos_in, pos_ref), (hrow_in, hrow_ref), (keep_in, keep_ref), (owner_in, owner_ref)
        ))
    ]
    h_copy.start()
    for copy in small:
        copy.start()
    p_copy.start()

    h_copy.wait()
    pairs = listed_h // 2
    halves = ([], [])
    for t in range(pairs):
        a, b = wide(hown[t]), wide(hown[pairs + t])
        halves[0].append(jnp.where(left, a, swapped(b)).astype(jnp.bfloat16))
        halves[1].append(jnp.where(left, swapped(a), b).astype(jnp.bfloat16))
    for k in range(HALVES):
        hall[k, me_c] = jnp.concatenate(halves[k], axis=0).reshape(hall.shape[2:])
    pl.semaphore_wait(barrier, cols + rows - 2)

    def first_copy(k, step):
        piece = hall.at[k, me_c, lax.div(me_r, 2), core]
        return pltpu.make_async_remote_copy(
            src_ref=piece, dst_ref=piece,
            send_sem=move_send.at[k * cols + step, 0], recv_sem=move_recv.at[k * cols + step, 0],
            device_id=(me_r, target(step)), device_id_type=MESH,
        )

    def plane_copy(k, step, place, onto):
        piece = hall.at[k, origin(step), lax.div(pieces[place], 2), core]
        return pltpu.make_async_remote_copy(
            src_ref=piece, dst_ref=piece,
            send_sem=move_send.at[k * cols + step, onto],
            recv_sem=move_recv.at[k * cols + step, onto],
            device_id=(pieces[onto], me_c), device_id_type=MESH,
        )

    def core_copy(k, step, side):
        held = hall.at[k, origin(step), :, side]
        return pltpu.make_async_remote_copy(
            src_ref=held, dst_ref=held,
            send_sem=core_send.at[k * cols + step], recv_sem=core_recv.at[k * cols + step],
            device_id=(partner, me_c), device_id_type=MESH,
        )

    for k in range(HALVES):
        for step in range(1, cols):
            first_copy(k, step).start()
    for copy in small:
        copy.wait()

    width = table.shape[-1]
    lane = lax.broadcasted_iota(jnp.int32, (8, width), 1)
    line = lax.broadcasted_iota(jnp.int32, (8, width), 0)
    wanted = repeat(
        hrow_ref.shape[0], lambda m, held: jnp.where(lane == m, hrow_ref[m], held),
        jnp.full((8, width), -1, jnp.int32),
    )
    wanted = jnp.where(wanted < 0, -1, wanted + line * KB)
    found = repeat(
        listed_p, lambda q, held: jnp.where(wanted == pos_ref[q], q, held),
        jnp.full((8, width), listed_p, jnp.int32),
    )
    filled = jnp.full((8, width), blocks, jnp.int32)
    count = jnp.zeros((8, width), jnp.int32) + rb
    for b in range(blocks):
        r, j = b // ncb, b % ncb
        hit = lane == owner_ref[r, 0, j]
        taken = jnp.where(keep_ref[r, j] == 1, b, blocks)
        filled = jnp.where(hit & (count == line), taken, filled)
        count = count + hit.astype(jnp.int32)
    table[...] = jnp.where(line < rb, found, filled)
    t_copy = pltpu.make_async_copy(table, stable, local_sem.at[2])
    t_copy.start()
    pv[listed_p] = jnp.zeros((block, block), jnp.bfloat16)
    for k in range(HALVES):
        for s in range(SEND_CAP):
            kept[k, s, blocks] = jnp.zeros((block, block), jnp.bfloat16)

    def multiply(k, column):
        panel = hall[k, column].reshape(pairs * block, block)
        parts = []
        for first in (0, pairs):
            sides = []
            for r in range(rb):
                sides.append(jnp.concatenate(
                    [pv[stable[r, column * listed_h + first + n]] for n in range(pairs)], axis=1
                ))
            parts.append(jnp.dot(
                jnp.concatenate(sides, axis=0), panel, preferred_element_type=jnp.float32
            ))
        for r in range(rb):
            low, high = [part[r * block:(r + 1) * block] for part in parts]
            total = jnp.where(left, low, high)
            total = total + swapped(total)
            zero = jnp.zeros_like(total)
            kept[k, 0, r * ncb + column] = jnp.where(left, total, zero).astype(jnp.bfloat16)
            kept[k, 1, r * ncb + column] = jnp.where(left, zero, total).astype(jnp.bfloat16)

    def deal_copy(k, step):
        owner = xor(me_r, step)
        return pltpu.make_async_remote_copy(
            src_ref=outgoing.at[k, owner], dst_ref=received.at[k, me_r],
            send_sem=deal_send.at[k * rows + step], recv_sem=deal_recv.at[k * rows + step],
            device_id=(owner, me_c), device_id_type=MESH,
        )

    def deal(k):
        for step in range(rows - 1, -1, -1):
            owner = xor(me_r, step)
            tile = kept[k, 0, stable[rb, owner]] + kept[k, 1, stable[rb + 1, owner]]
            if step:
                outgoing[k, owner] = tile
                deal_copy(k, step).start()
            else:
                received[k, me_r] = tile

    for k in range(HALVES):
        for step in range(1, cols):
            first_copy(k, step).wait_recv()
            for place in range(places - 1, 0, -1):
                plane_copy(k, step, 0, place).start()
    t_copy.wait()
    p_copy.wait()
    for k in range(HALVES):
        multiply(k, me_c)
    for k in range(HALVES):
        for step in range(1, cols):
            for place in range(1, places):
                plane_copy(k, step, place, place).wait_recv()
            core_copy(k, step, core).start()
    for k in range(HALVES):
        for step in range(1, cols):
            core_copy(k, step, 1 - core).wait_recv()
            multiply(k, origin(step))
        deal(k)

    for k in range(HALVES):
        for step in range(1, cols):
            first_copy(k, step).wait_send()
            for place in range(1, places):
                plane_copy(k, step, 0, place).wait_send()
            core_copy(k, step, core).wait_send()
    for step in range(rows):
        sender = xor(me_r, step)
        if step:
            for k in range(HALVES):
                deal_copy(k, step).wait_send()
                deal_copy(k, step).wait_recv()
        a, b = wide(received[0, sender]), wide(received[1, sender])
        out_ref[sender, 0] = jnp.where(left, a, swapped(b)).astype(jnp.bfloat16)
        out_ref[sender, 1] = jnp.where(left, swapped(a), b).astype(jnp.bfloat16)


def local(rows, cols, p_blocks, p_positions, h_blocks, h_rows, keep_mask, owner_ids):
    listed_p, block = p_blocks.shape[:2]
    listed_h = h_blocks.shape[0]
    blocks = keep_mask.size
    depth = listed_h * block // rows // HALVES
    places = rows // 2
    width = -(-max(h_rows.shape[0], rows) // LANES) * LANES
    hbm = pl.BlockSpec(memory_space=pltpu.HBM)
    dma = pltpu.SemaphoreType.DMA
    return pl.pallas_call(
        functools.partial(kernel, rows, cols),
        out_shape=pltpu.VMEM((rows, SEND_CAP, block, block), jnp.bfloat16),
        in_specs=[hbm] * 6,
        out_specs=pl.BlockSpec(memory_space=pltpu.VMEM),
        scratch_shapes=[
            pltpu.SMEM(p_positions.shape, jnp.int32),
            pltpu.SMEM(h_rows.shape, jnp.int32),
            pltpu.SMEM(keep_mask.shape, jnp.int32),
            pltpu.SMEM((keep_mask.shape[0], 1, keep_mask.shape[1]), jnp.int32),
            pltpu.VMEM((listed_p + 1, block, block), jnp.bfloat16),
            pltpu.VMEM(h_blocks.shape, jnp.bfloat16),
            pltpu.VMEM((HALVES, cols, rows // 2, 2, depth, block), jnp.bfloat16),
            pltpu.VMEM((HALVES, SEND_CAP, blocks + 1, block, block), jnp.bfloat16),
            pltpu.VMEM((HALVES, rows, block, block), jnp.bfloat16),
            pltpu.VMEM((HALVES, rows, block, block), jnp.bfloat16),
            pltpu.VMEM((8, width), jnp.int32),
            pltpu.SMEM((8, width), jnp.int32),
            dma((8,)),
            dma((HALVES * cols, places)),
            dma((HALVES * cols, places)),
            dma((HALVES * cols,)),
            dma((HALVES * cols,)),
            dma((HALVES * rows,)),
            dma((HALVES * rows,)),
        ],
        compiler_params=pltpu.CompilerParams(
            collective_id=0, has_side_effects=True, vmem_limit_bytes=40 * 1024 * 1024
        ),
    )(*[
        pltpu.with_memory_space_constraint(given, pltpu.HBM) for given in (
            p_positions, h_rows, keep_mask, jnp.transpose(owner_ids, (0, 2, 1)), p_blocks,
            h_blocks,
        )
    ])


def solution(mesh):
    return jax.shard_map(
        functools.partial(local, mesh.shape["row"], mesh.shape["col"]),
        mesh=mesh,
        in_specs=(
            P(("row", "col"), None, None),
            P(("row", "col")),
            P("col", None, None),
            P(),
            P(("row", "col"), None),
            P(("row", "col"), None, None),
        ),
        out_specs=P(("row", "col"), None, None, None),
        check_vma=False,
    )
```

```python
import functools

import jax
import jax.numpy as jnp
from jax import lax
from jax.experimental import pallas as pl
from jax.experimental.pallas import tpu as pltpu
from jax.sharding import PartitionSpec as P

KB = 64
SEND_CAP = 2
LANES = 128
UNROLL = 64
MESH = pl.DeviceIdType.MESH


def repeat(count, body, init=None):
    if count <= UNROLL:
        for i in range(count):
            init = body(i, init)
        return init
    return lax.fori_loop(0, count, body, init)


def xor(value, mask):
    bit = 1
    while bit <= mask:
        if mask & bit:
            value = value + bit * (1 - 2 * lax.rem(lax.div(value, bit), 2))
        bit *= 2
    return value


def kernel(
    rows, cols, pos_in, hrow_in, keep_in, owner_in, p_ref, h_ref, out_ref,
    pos_ref, hrow_ref, keep_ref, owner_ref, pv, hall, kept, outgoing, table, stable,
    local_sem, move_send, move_recv, core_send, core_recv, deal_send, deal_recv,
):
    me_r, me_c = lax.axis_index("row"), lax.axis_index("col")
    core = lax.rem(me_r, 2)
    listed_p = p_ref.shape[0]
    block = p_ref.shape[-1]
    rb, ncb = keep_ref.shape
    blocks = rb * ncb
    listed_h = hrow_ref.shape[0] // cols
    dims = rows.bit_length() - 2
    places = 2**dims
    power = cols & (cols - 1) == 0

    def target(step):
        return xor(me_c, step) if power else lax.rem(me_c + step, cols)

    def origin(step):
        return xor(me_c, step) if power else lax.rem(me_c + cols - step, cols)

    strides = []
    for i in range(dims):
        first, second = 2 ** (dims - i), 2 ** (i + 1)
        moves = [stride * (1 - 2 * lax.rem(lax.div(me_r, stride), 2)) for stride in (first, second)]
        strides.append(moves[0] + core * (moves[1] - moves[0]))
    pieces = [me_r]
    for stride in strides:
        pieces = pieces + [piece + stride for piece in pieces]
    toward = 1 - 2 * core
    partner = me_r + toward

    barrier = pltpu.get_barrier_semaphore()
    for step in range(1, cols):
        pl.semaphore_signal(barrier, inc=1, device_id=(me_r, target(step)), device_id_type=MESH)
    for step in range(1, rows):
        pl.semaphore_signal(barrier, inc=1, device_id=(xor(me_r, step), me_c), device_id_type=MESH)

    p_copy = pltpu.make_async_copy(p_ref, pv.at[pl.ds(0, listed_p)], local_sem.at[0])
    h_copy = pltpu.make_async_copy(h_ref, hall.at[me_c], local_sem.at[1])
    small = [
        pltpu.make_async_copy(given, held, local_sem.at[4 + i])
        for i, (given, held) in enumerate((
            (pos_in, pos_ref), (hrow_in, hrow_ref), (keep_in, keep_ref), (owner_in, owner_ref)
        ))
    ]
    for copy in small:
        copy.start()
    h_copy.start()
    p_copy.start()
    pl.semaphore_wait(barrier, cols + rows - 2)

    def first_copy(step):
        return pltpu.make_async_remote_copy(
            src_ref=h_ref.at[lax.div(me_r, 2), core], dst_ref=hall.at[me_c, lax.div(me_r, 2), core],
            send_sem=move_send.at[step, 0], recv_sem=move_recv.at[step, 0],
            device_id=(me_r, target(step)), device_id_type=MESH,
        )

    def plane_copy(step, place, onto, to_row, sends, recvs):
        piece = hall.at[origin(step), lax.div(pieces[place], 2), core]
        return pltpu.make_async_remote_copy(
            src_ref=piece, dst_ref=piece,
            send_sem=sends.at[step, onto], recv_sem=recvs.at[step, onto],
            device_id=(to_row, me_c), device_id_type=MESH,
        )

    def core_copy(step, side):
        held = hall.at[origin(step), :, side]
        return pltpu.make_async_remote_copy(
            src_ref=held, dst_ref=held,
            send_sem=core_send.at[step], recv_sem=core_recv.at[step],
            device_id=(partner, me_c), device_id_type=MESH,
        )

    for step in range(cols - 1, 0, -1):
        first_copy(step).start()
    for copy in small:
        copy.wait()

    width = table.shape[-1]
    lane = lax.broadcasted_iota(jnp.int32, (8, width), 1)
    line = lax.broadcasted_iota(jnp.int32, (8, width), 0)
    wanted = repeat(
        hrow_ref.shape[0], lambda m, held: jnp.where(lane == m, hrow_ref[m], held),
        jnp.full((8, width), -1, jnp.int32),
    )
    wanted = jnp.where(wanted < 0, -1, wanted + line * KB)
    found = repeat(
        listed_p, lambda q, held: jnp.where(wanted == pos_ref[q], q, held),
        jnp.full((8, width), listed_p, jnp.int32),
    )
    filled = jnp.full((8, width), blocks, jnp.int32)
    count = jnp.zeros((8, width), jnp.int32) + rb
    for b in range(blocks):
        r, j = b // ncb, b % ncb
        hit = lane == owner_ref[r, 0, j]
        taken = jnp.where(keep_ref[r, j] == 1, b, blocks)
        filled = jnp.where(hit & (count == line), taken, filled)
        count = count + hit.astype(jnp.int32)
    table[...] = jnp.where(line < rb, found, filled)
    t_copy = pltpu.make_async_copy(table, stable, local_sem.at[2])
    t_copy.start()
    pv[listed_p] = jnp.zeros((block, block), jnp.bfloat16)
    kept[blocks] = jnp.zeros((block, block), jnp.bfloat16)

    def multiply(column):
        sides = []
        for r in range(rb):
            sides.append(jnp.concatenate(
                [pv[stable[r, column * listed_h + n]] for n in range(listed_h)], axis=1
            ))
        panel = hall[column].reshape(listed_h * block, block)
        product = jnp.dot(
            jnp.concatenate(sides, axis=0), panel, preferred_element_type=jnp.float32
        ).astype(jnp.bfloat16)
        for r in range(rb):
            kept[r * ncb + column] = product[r * block:(r + 1) * block]

    for step in range(1, cols):
        first_copy(step).wait_recv()
        for place in range(places - 1, 0, -1):
            plane_copy(step, 0, place, pieces[place], move_send, move_recv).start()
    t_copy.wait()
    p_copy.wait()
    h_copy.wait()
    multiply(me_c)
    for step in range(1, cols + 2):
        if step < cols:
            for place in range(1, places):
                plane_copy(step, place, place, me_r, move_send, move_recv).wait_recv()
            core_copy(step, core).start()
        if step > 2:
            core_copy(step - 2, 1 - core).wait_recv()
            multiply(origin(step - 2))

    def deal(step):
        owner = xor(me_r, step)
        return pltpu.make_async_remote_copy(
            src_ref=outgoing.at[owner], dst_ref=out_ref.at[me_r],
            send_sem=deal_send.at[step], recv_sem=deal_recv.at[step],
            device_id=(owner, me_c), device_id_type=MESH,
        )

    for step in range(rows - 1, -1, -1):
        owner = xor(me_r, step)
        for s in range(SEND_CAP):
            outgoing[owner, s] = kept[stable[rb + s, owner]]
        if step:
            deal(step).start()
    own = pltpu.make_async_copy(outgoing.at[me_r], out_ref.at[me_r], local_sem.at[3])
    own.start()
    for step in range(1, cols):
        first_copy(step).wait_send()
        for place in range(1, places):
            plane_copy(step, 0, place, me_r, move_send, move_recv).wait_send()
        core_copy(step, core).wait_send()
    for step in range(rows - 1, 0, -1):
        deal(step).wait_send()
        deal(step).wait_recv()
    own.wait()


def local(rows, cols, p_blocks, p_positions, h_blocks, h_rows, keep_mask, owner_ids):
    listed_p, block = p_blocks.shape[:2]
    listed_h = h_blocks.shape[0]
    blocks = keep_mask.size
    depth = listed_h * block // rows
    places = rows // 2
    width = -(-max(h_rows.shape[0], rows) // LANES) * LANES
    hbm = pl.BlockSpec(memory_space=pltpu.HBM)
    anywhere = pl.BlockSpec(memory_space=pl.ANY)
    dma = pltpu.SemaphoreType.DMA
    return pl.pallas_call(
        functools.partial(kernel, rows, cols),
        out_shape=pltpu.VMEM((rows, SEND_CAP, block, block), jnp.bfloat16),
        in_specs=[hbm] * 6,
        out_specs=anywhere,
        scratch_shapes=[
            pltpu.SMEM(p_positions.shape, jnp.int32),
            pltpu.SMEM(h_rows.shape, jnp.int32),
            pltpu.SMEM(keep_mask.shape, jnp.int32),
            pltpu.SMEM((keep_mask.shape[0], 1, keep_mask.shape[1]), jnp.int32),
            pltpu.VMEM((listed_p + 1, block, block), jnp.bfloat16),
            pltpu.VMEM((cols, rows // 2, 2, depth, block), jnp.bfloat16),
            pltpu.VMEM((blocks + 1, block, block), jnp.bfloat16),
            pltpu.VMEM((rows, SEND_CAP, block, block), jnp.bfloat16),
            pltpu.VMEM((8, width), jnp.int32),
            pltpu.SMEM((8, width), jnp.int32),
            dma((8,)),
            dma((cols, places)),
            dma((cols, places)),
            dma((cols,)),
            dma((cols,)),
            dma((rows,)),
            dma((rows,)),
        ],
        compiler_params=pltpu.CompilerParams(
            collective_id=0, has_side_effects=True, vmem_limit_bytes=40 * 1024 * 1024
        ),
    )(*[
        pltpu.with_memory_space_constraint(given, pltpu.HBM) for given in (
            p_positions, h_rows, keep_mask, jnp.transpose(owner_ids, (0, 2, 1)), p_blocks,
            h_blocks.reshape(rows // 2, 2, depth, block),
        )
    ])


def solution(mesh):
    return jax.shard_map(
        functools.partial(local, mesh.shape["row"], mesh.shape["col"]),
        mesh=mesh,
        in_specs=(
            P(("row", "col"), None, None),
            P(("row", "col")),
            P("col", None, None),
            P(),
            P(("row", "col"), None),
            P(("row", "col"), None, None),
        ),
        out_specs=P(("row", "col"), None, None, None),
        check_vma=False,
    )
```
